512 devices in a mesh: seq: 64 (over z, x), head: 8 (over y, core).
Axes of the slice: x: 4, y: 4, z: 16, core: 2. Of those that a mesh axis runs over, the one named last changes fastest.
Arguments:
- queries: bfloat16 [2, 8192, 16, 128], P(None, 'seq', 'head'), may hold values from -6 to 6
- keys: bfloat16 [2, 8192, 16, 128], P(None, 'seq', 'head'), may hold values from -6 to 6
- values: bfloat16 [2, 8192, 16, 128], P(None, 'seq', 'head'), may hold values from -6 to 6
- teacher: bfloat16 [2, 8192, 16, 128], P(None, 'seq', 'head'), may hold values from -4 to 4
- query_map: bfloat16 [128, 128], replicated, may hold values from -1.5 to 1.5
- key_map: bfloat16 [128, 128], replicated, may hold values from -1.5 to 1.5
Outputs:
- grad_query_map: float32 [128, 128], replicated
- grad_key_map: float32 [128, 128], replicated
The draws below stay inside these ranges and needn't reach their ends.
All inputs are finite; a program needn't handle non-finite values.
Results may differ from the reference program's by a relative error of at most 0.0003.
Values sent between devices are 32-bit elements; how exact they have to be, the bound alone decides.
A program may use at most 128 MiB of HBM per device.

```python
import jax
import jax.numpy as jnp
from jax import lax

H = 16
DH = 128
F = 128
SEQS = 2
TOK_DEV = 128
LENGTH = 8192
N_SEQ = 64


def block_scale(stream_key, shape, cuts, least, top_value):
    def one(axis_at, shards_of):
        heights = jax.random.uniform(jax.random.fold_in(jax.random.fold_in(stream_key, 6), axis_at), (shards_of,), jnp.float32, least / len(cuts), top_value / len(cuts))
        return jnp.repeat(jnp.exp(heights), shape[axis_at] // shards_of).reshape((-1,) + (1,) * (len(shape) - axis_at - 1))

    loudness = one(*cuts[0])
    for cut in cuts[1:]:
        loudness = loudness * one(*cut)
    return loudness


def centred(own_key, shape, width, most, cuts=(), kind=jnp.bfloat16):
    values = jax.random.normal(own_key, shape, jnp.float32) * width
    if len(cuts) > 0:
        values = block_scale(own_key, shape, cuts, -0.22, 0.18) * values
    return jnp.clip(values, min=-most, max=most).astype(kind)


def setup_inputs(seed: int = 0) -> dict:
    arg_keys = jax.random.split(jax.random.key(seed), 7)
    return {
        "queries": centred(arg_keys[0], (SEQS, LENGTH, H, DH), 1.0, 6.0, ((1, 64), (2, 8))),
        "keys": centred(arg_keys[1], (SEQS, LENGTH, H, DH), 1.0, 6.0, ((1, 64), (2, 8))),
        "values": centred(arg_keys[2], (SEQS, LENGTH, H, DH), 1.0, 6.0, ((1, 64), (2, 8))),
        "teacher": centred(arg_keys[3], (SEQS, LENGTH, H, DH), 0.5, 4.0, ((1, 64), (2, 8))),
        "query_map": centred(arg_keys[4], (DH, F), 16 ** -0.5, 1.5),
        "key_map": centred(arg_keys[5], (DH, F), 16 ** -0.5, 1.5),
    }


HIGH = lax.Precision.HIGHEST


def feature(inputs, matrix):
    logits = jnp.dot(inputs, matrix, preferred_element_type=jnp.float32)
    rising = jnp.exp(logits)
    falling = jnp.exp(-logits)
    return jnp.concatenate([rising / jnp.sum(rising, -1, keepdims=True), falling / jnp.sum(falling, -1, keepdims=True)], -1)


def feature_back(phi, dphi):
    half_width = phi.shape[-1] // 2
    part_up = phi[..., :half_width]
    part_down = phi[..., half_width:]
    grad_up = dphi[..., :half_width]
    grad_down = dphi[..., half_width:]
    return part_up * (grad_up - jnp.sum(part_up * grad_up, -1, keepdims=True)) - part_down * (grad_down - jnp.sum(part_down * grad_down, -1, keepdims=True))


def exclusive(stack):
    running = jnp.cumsum(stack, 0)
    return jnp.concatenate([jnp.zeros_like(stack[:1]), running[:-1]], 0)


def one_pair(pieces, query_map, key_map):
    query, key_in, value_in, target_in = pieces
    query_phi = feature(query, query_map)
    key_phi = feature(key_in, key_map)
    value_full = value_in.astype(jnp.float32)
    target_full = target_in.astype(jnp.float32)
    local_state = jnp.einsum('ntf,ntd->nfd', key_phi, value_full, precision=HIGH)
    local_norm = jnp.sum(key_phi, 1)
    prefix_state = exclusive(local_state)
    prefix_norm = exclusive(local_norm)
    size_t = query.shape[1]
    causal = (lax.broadcasted_iota(jnp.int32, (size_t, size_t), 0) >= lax.broadcasted_iota(jnp.int32, (size_t, size_t), 1)).astype(jnp.float32)

    def block_step(blocks):
        qphi, kphi, vfull, target, state, norm = blocks
        scores = jnp.dot(qphi, kphi.T, precision=HIGH) * causal
        numerator = jnp.dot(scores, vfull, precision=HIGH) + jnp.dot(qphi, state, precision=HIGH)
        denominator = jnp.sum(scores, 1) + jnp.dot(qphi, norm, precision=HIGH)
        output = numerator / denominator[:, None]
        misfit = output - target
        grad_num = misfit / denominator[:, None]
        grad_den = -jnp.sum(misfit * output, 1) / denominator
        mixed_grad = (jnp.dot(grad_num, vfull.T, precision=HIGH) + grad_den[:, None]) * causal
        query_dphi = jnp.dot(mixed_grad, kphi, precision=HIGH) + jnp.dot(grad_num, state.T, precision=HIGH) + grad_den[:, None] * norm[None, :]
        key_inner = jnp.dot(mixed_grad.T, qphi, precision=HIGH)
        return query_dphi, key_inner, jnp.dot(qphi.T, grad_num, precision=HIGH), jnp.dot(grad_den, qphi, precision=HIGH)

    query_dphi, key_inner, back_state, back_norm = lax.map(block_step, (query_phi, key_phi, value_full, target_full, prefix_state, prefix_norm))
    suffix_state = exclusive(back_state[::-1])[::-1]
    suffix_norm = exclusive(back_norm[::-1])[::-1]
    key_dphi = key_inner + jnp.einsum('ntd,nfd->ntf', value_full, suffix_state, precision=HIGH) + suffix_norm[:, None, :]
    grad_aq = feature_back(query_phi, query_dphi)
    grad_ak = feature_back(key_phi, key_dphi)
    grad_q = jnp.einsum('ntd,ntf->df', query.astype(jnp.float32), grad_aq, precision=HIGH)
    grad_k = jnp.einsum('ntd,ntf->df', key_in.astype(jnp.float32), grad_ak, precision=HIGH)
    return grad_q, grad_k


def reference(queries, keys, values, teacher, query_map, key_map):
    def arrange(array):
        return jnp.transpose(array, (0, 2, 1, 3)).reshape(SEQS * H, N_SEQ, TOK_DEV, DH)

    def pair_step(pieces):
        return one_pair(pieces, query_map, key_map)

    grad_q, grad_k = lax.map(pair_step, (arrange(queries), arrange(keys), arrange(values), arrange(teacher)))
    return jnp.sum(grad_q, 0), jnp.sum(grad_k, 0)
```

```python
import jax
import jax.numpy as jnp
from jax import lax
from jax.experimental import pallas as pl
from jax.experimental.pallas import tpu as pltpu
from jax.sharding import PartitionSpec as P

MESH = pl.DeviceIdType.MESH
F32 = jnp.float32
BF16 = jnp.bfloat16

NZ, NX, NY, NC = 16, 4, 4, 2
TOK = 128
DH = 128
F2 = 256
LOC = NX * TOK
FC = F2 // NZ
Z_FAR_FIRST = (8, 7, 9, 6, 10, 5, 11, 4, 12, 3, 13, 2, 14, 1, 15)
X_FAR_FIRST = (2, 1, 3)
XY_FAR_FIRST = tuple(
    sorted(
        ((dx, dy) for dx in range(NX) for dy in range(NY) if dx or dy),
        key=lambda d: -(min(d[0], NX - d[0]) + min(d[1], NY - d[1])),
    )
)

NN = (((1,), (0,)), ((), ()))
NT = (((1,), (1,)), ((), ()))
TN = (((0,), (0,)), ((), ()))


def split(a):
    high = a.astype(BF16)
    return high, (a - high.astype(F32)).astype(BF16)


def mm(a, b, dims):
    return lax.dot_general(a, b, dims, preferred_element_type=F32)


def mm3(a, b, dims):
    return mm(a[0], b[0], dims) + (mm(a[0], b[1], dims) + mm(a[1], b[0], dims))


def mm2(a, b, dims):
    return mm(a[0], b, dims) + mm(a[1], b, dims)


def feature(inputs, matrix):
    logits = mm(inputs, matrix, NN)
    rising = jnp.exp(logits)
    falling = jnp.exp(-logits)
    return jnp.concatenate(
        [
            rising / jnp.sum(rising, -1, keepdims=True),
            falling / jnp.sum(falling, -1, keepdims=True),
        ],
        -1,
    )


def feature_back(phi, dphi):
    half = phi.shape[-1] // 2
    up, down = phi[:, :half], phi[:, half:]
    grad_up, grad_down = dphi[:, :half], dphi[:, half:]
    return up * (grad_up - jnp.sum(up * grad_up, -1, keepdims=True)) - down * (
        grad_down - jnp.sum(down * grad_down, -1, keepdims=True)
    )


def kernel(
    k_hbm,
    v_hbm,
    q_hbm,
    t_hbm,
    qmap_hbm,
    kmap_hbm,
    out_ref,
    raw,
    maps,
    wide,
    stage,
    held,
    state,
    norms,
    got_state,
    got_norm,
    totals,
    entering,
    part,
    got_part,
    sums,
    got_sum,
    got_core,
    load_sem,
    x_send,
    x_recv,
    z_send,
    z_recv,
    n_send,
    n_recv,
    r_send,
    r_recv,
    c_send,
    c_recv,
    g_send,
    g_recv,
):
    seq, head = lax.axis_index("seq"), lax.axis_index("head")
    z, x = seq // NX, seq % NX
    y, core = head // NC, head % NC

    def at_z(d):
        other = (z + d) % NZ
        return other, (other * NX + x, head)

    def at_x(d):
        other = (x + d) % NX
        return other, (z * NX + other, head)

    def at_xy(d):
        ox, oy = (x + d[0]) % NX, (y + d[1]) % NY
        return ox * NY + oy, (z * NX + ox, oy * NC + core)

    other_core = (seq, y * NC + (1 - core))

    loads = []
    for i, (src, dst) in enumerate(
        (
            (k_hbm, raw.at[0]),
            (v_hbm, raw.at[1]),
            (kmap_hbm, maps.at[0]),
            (q_hbm, raw.at[2]),
            (t_hbm, raw.at[3]),
            (qmap_hbm, maps.at[1]),
        )
    ):
        load = pltpu.make_async_copy(src, dst, load_sem.at[i])
        load.start()
        loads.append(load)

    barrier = pltpu.get_barrier_semaphore()
    partners = [at_x(d)[1] for d in X_FAR_FIRST]
    partners += [at_z(d)[1] for d in Z_FAR_FIRST]
    partners += [at_xy(d)[1] for d in XY_FAR_FIRST if d[1]]
    partners += [other_core]
    for partner in partners:
        pl.semaphore_signal(barrier, inc=1, device_id=partner, device_id_type=MESH)

    sent = []

    def send(src, dst, send_sem, recv_sem, device):
        copy = pltpu.make_async_remote_copy(
            src_ref=src,
            dst_ref=dst,
            send_sem=send_sem,
            recv_sem=recv_sem,
            device_id=device,
            device_id_type=MESH,
        )
        copy.start()
        sent.append(copy)
        return copy

    def widen(i):
        wide[i] = raw[i].astype(F32)
        for b in range(2):
            for h in range(2):
                stage[i, b * 2 + h] = wide[i, pl.ds(b * 2 * TOK + h, TOK, stride=2), :]
        held[i, x] = stage[i, x]

    loads[0].wait()
    widen(0)
    loads[1].wait()
    widen(1)
    pl.semaphore_wait(barrier, len(partners))

    x_copies = [[], [], [], []]

    def send_x(i):
        for d in X_FAR_FIRST:
            other, device = at_x(d)
            x_copies[i].append(
                send(stage.at[i, other], held.at[i, x], x_send.at[i, d - 1], x_recv.at[i, d - 1], device)
            )

    send_x(0)
    send_x(1)
    loads[3].wait()
    widen(2)
    send_x(2)
    loads[4].wait()
    widen(3)
    send_x(3)
    loads[2].wait()
    loads[5].wait()

    def receive_x(i):
        for copy in x_copies[i]:
            copy.wait_recv()
        return held[i].reshape(LOC, DH)

    def scatter_z(scan, full_state, full_norm):
        state[scan] = full_state.reshape(NZ, FC, DH)
        norms[scan] = full_norm
        copies = []
        for d in Z_FAR_FIRST:
            other, device = at_z(d)
            copies.append(
                send(state.at[scan, other], got_state.at[scan, z], z_send.at[2 * scan, d - 1], z_recv.at[2 * scan, d - 1], device)
            )
            copies.append(
                send(norms.at[scan], got_norm.at[scan, z], n_send.at[scan, d - 1], n_recv.at[scan, d - 1], device)
            )
        got_state[scan, z] = state[scan, z]
        got_norm[scan, z] = norms[scan]
        return copies

    def return_z(scan, copies, reverse):
        for copy in copies:
            copy.wait_recv()
        order = range(NZ - 1, -1, -1) if reverse else range(NZ)
        running = jnp.zeros((FC, DH), F32)
        for one in order:
            totals[scan, one] = running
            running = running + got_state[scan, one]
        copies = []
        for d in Z_FAR_FIRST:
            other, device = at_z(d)
            copies.append(
                send(totals.at[scan, other], entering.at[scan, z], z_send.at[2 * scan + 1, d - 1], z_recv.at[2 * scan + 1, d - 1], device)
            )
        entering[scan, z] = totals[scan, z]
        norm = jnp.zeros((1, F2), F32)
        for one in order:
            before = one > z if reverse else one < z
            norm = norm + jnp.where(before, got_norm[scan, one], 0.0)
        return copies, norm

    def receive_z(scan, copies):
        for copy in copies:
            copy.wait_recv()
        return entering[scan].reshape(F2, DH)

    keys = receive_x(0).astype(BF16)
    key_phi = feature(keys, maps[0])
    kphi = split(key_phi)
    values = receive_x(1).astype(BF16)
    copies = scatter_z(0, mm2(kphi, values, TN), jnp.sum(key_phi, 0, keepdims=True))

    queries = receive_x(2).astype(BF16)
    query_phi = feature(queries, maps[1])
    qphi = split(query_phi)
    causal = lax.broadcasted_iota(jnp.int32, (LOC, LOC), 0) >= lax.broadcasted_iota(
        jnp.int32, (LOC, LOC), 1
    )
    scores = jnp.where(causal, mm3(qphi, kphi, NT), 0.0)
    inner_num = mm2(split(scores), values, NN)
    inner_den = jnp.sum(scores, 1, keepdims=True)
    target = receive_x(3)

    copies, prefix_norm = return_z(0, copies, False)
    denominator = inner_den + jnp.sum(query_phi * prefix_norm, 1, keepdims=True)
    prefix = split(receive_z(0, copies))

    output = (inner_num + mm3(qphi, prefix, NN)) / denominator
    misfit = output - target
    grad_num = misfit / denominator
    grad_den = -jnp.sum(misfit * output, 1, keepdims=True) / denominator
    gnum = split(grad_num)
    copies = scatter_z(
        1, mm3(qphi, gnum, TN), jnp.sum(query_phi * grad_den, 0, keepdims=True)
    )

    mixed = split(jnp.where(causal, mm(gnum[0], values, NT) + mm(gnum[1], values, NT) + grad_den, 0.0))
    query_dphi = mm3(mixed, kphi, NN) + mm3(gnum, prefix, NT) + grad_den * prefix_norm
    key_inner = mm3(mixed, qphi, TN)
    grad_aq = split(feature_back(query_phi, query_dphi))
    grad_q = mm(queries, grad_aq[0], TN) + mm(queries, grad_aq[1], TN)
    part[:, 0] = grad_q.reshape(16, 8, DH)

    copies, suffix_norm = return_z(1, copies, True)
    suffix = split(receive_z(1, copies))
    key_dphi = key_inner + mm(values, suffix[0], NT) + mm(values, suffix[1], NT) + suffix_norm
    grad_ak = split(feature_back(key_phi, key_dphi))
    grad_k = mm(keys, grad_ak[0], TN) + mm(keys, grad_ak[1], TN)
    part[:, 1] = grad_k.reshape(16, 8, DH)

    mine = x * NY + y
    copies = []
    for i, d in enumerate(XY_FAR_FIRST):
        other, device = at_xy(d)
        copies.append(send(part.at[other], got_part.at[mine], r_send.at[i], r_recv.at[i], device))
    got_part[mine] = part[mine]
    for copy in copies:
        copy.wait_recv()
    sums[0] = jnp.sum(got_part[...], 0)
    copy = send(sums.at[0], got_core, c_send.at[0], c_recv.at[0], other_core)
    copy.wait_recv()
    sums[1] = sums[0] + got_core[...]
    copies = []
    for d in Z_FAR_FIRST:
        other, device = at_z(d)
        copies.append(send(sums.at[1], got_sum.at[z], r_send.at[14 + d], r_recv.at[14 + d], device))
    got_sum[z] = sums[1]
    for copy in copies:
        copy.wait_recv()
    sums[2] = jnp.sum(got_sum[...], 0)
    copies = []
    for i, d in enumerate(XY_FAR_FIRST):
        other, device = at_xy(d)
        copies.append(send(sums.at[2], out_ref.at[mine], g_send.at[i], g_recv.at[i], device))
    out_ref[mine] = sums[2]
    for copy in copies:
        copy.wait_recv()
    for copy in sent:
        copy.wait_send()


def per_device(queries, keys, values, teacher, query_map, key_map):
    def flat(a):
        return a.reshape(-1, DH)

    out = pl.pallas_call(
        kernel,
        out_shape=jax.ShapeDtypeStruct((16, 2, 8, DH), F32),
        in_specs=[pl.BlockSpec(memory_space=pl.ANY)] * 6,
        out_specs=pl.BlockSpec(memory_space=pltpu.VMEM),
        scratch_shapes=[
            pltpu.VMEM((4, 4 * TOK, DH), BF16),
            pltpu.VMEM((2, DH, DH), BF16),
            pltpu.VMEM((4, 4 * TOK, DH), F32),
            pltpu.VMEM((4, 4, TOK, DH), F32),
            pltpu.VMEM((4, NX, TOK, DH), F32),
            pltpu.VMEM((2, NZ, FC, DH), F32),
            pltpu.VMEM((2, 1, F2), F32),
            pltpu.VMEM((2, NZ, FC, DH), F32),
            pltpu.VMEM((2, NZ, 1, F2), F32),
            pltpu.VMEM((2, NZ, FC, DH), F32),
            pltpu.VMEM((2, NZ, FC, DH), F32),
            pltpu.VMEM((16, 2, 8, DH), F32),
            pltpu.VMEM((16, 2, 8, DH), F32),
            pltpu.VMEM((3, 2, 8, DH), F32),
            pltpu.VMEM((NZ, 2, 8, DH), F32),
            pltpu.VMEM((2, 8, DH), F32),
            pltpu.SemaphoreType.DMA((6,)),
            pltpu.SemaphoreType.DMA((4, 3)),
            pltpu.SemaphoreType.DMA((4, 3)),
            pltpu.SemaphoreType.DMA((4, 15)),
            pltpu.SemaphoreType.DMA((4, 15)),
            pltpu.SemaphoreType.DMA((2, 15)),
            pltpu.SemaphoreType.DMA((2, 15)),
            pltpu.SemaphoreType.DMA((30,)),
            pltpu.SemaphoreType.DMA((30,)),
            pltpu.SemaphoreType.DMA((1,)),
            pltpu.SemaphoreType.DMA((1,)),
            pltpu.SemaphoreType.DMA((15,)),
            pltpu.SemaphoreType.DMA((15,)),
        ],
        compiler_params=pltpu.CompilerParams(
            collective_id=0, has_side_effects=True, vmem_limit_bytes=56 * 1024 * 1024
        ),
        name="hedgehog",
    )(flat(keys), flat(values), flat(queries), flat(teacher), query_map, key_map)
    return out[:, 0].reshape(DH, DH), out[:, 1].reshape(DH, DH)


def solution(mesh):
    split_spec = P(None, "seq", "head", None)
    return jax.shard_map(
        per_device,
        mesh=mesh,
        in_specs=(split_spec,) * 4 + (P(), P()),
        out_specs=(P(), P()),
        check_vma=False,
    )
```

```python
import jax
import jax.numpy as jnp
from jax import lax
from jax.experimental import pallas as pl
from jax.experimental.pallas import tpu as pltpu
from jax.sharding import PartitionSpec as P

MESH = pl.DeviceIdType.MESH
F32 = jnp.float32
BF16 = jnp.bfloat16

NZ, NX, NY, NC = 16, 4, 4, 2
TOK = 128
DH = 128
F2 = 256
LOC = NX * TOK
FC = F2 // NZ
Z_FAR_FIRST = (8, 7, 9, 6, 10, 5, 11, 4, 12, 3, 13, 2, 14, 1, 15)
X_FAR_FIRST = (2, 1, 3)
PLANE_FAR_FIRST = tuple(
    sorted(
        ((dx, dy, dc) for dx in range(NX) for dy in range(NY) for dc in range(NC) if dx or dy or dc),
        key=lambda d: -(min(d[0], NX - d[0]) + min(d[1], NY - d[1])),
    )
)
NP = NX * NY
ROWS = FC + 2

NN = (((1,), (0,)), ((), ()))
NT = (((1,), (1,)), ((), ()))
TN = (((0,), (0,)), ((), ()))


def split(a):
    high = a.astype(BF16)
    return high, (a - high.astype(F32)).astype(BF16)


def mm(a, b, dims):
    return lax.dot_general(a, b, dims, preferred_element_type=F32)


def mm3(a, b, dims):
    return mm(a[0], b[0], dims) + (mm(a[0], b[1], dims) + mm(a[1], b[0], dims))


def mm2(a, b, dims):
    return mm(a[0], b, dims) + mm(a[1], b, dims)


def feature(inputs, matrix):
    logits = mm(inputs, matrix, NN)
    rising = jnp.exp(logits)
    falling = jnp.exp(-logits)
    return jnp.concatenate(
        [
            rising / jnp.sum(rising, -1, keepdims=True),
            falling / jnp.sum(falling, -1, keepdims=True),
        ],
        -1,
    )


def feature_back(phi, dphi):
    half = phi.shape[-1] // 2
    up, down = phi[:, :half], phi[:, half:]
    grad_up, grad_down = dphi[:, :half], dphi[:, half:]
    return up * (grad_up - jnp.sum(up * grad_up, -1, keepdims=True)) - down * (
        grad_down - jnp.sum(down * grad_down, -1, keepdims=True)
    )


def kernel(
    k_hbm,
    v_hbm,
    q_hbm,
    t_hbm,
    qmap_hbm,
    kmap_hbm,
    out_ref,
    raw,
    maps,
    wide,
    stage,
    held,
    state,
    got_state,
    totals,
    entering,
    part,
    got_part,
    sums,
    got_sum,
    load_sem,
    x_send,
    x_recv,
    z_send,
    z_recv,
    r_send,
    r_recv,
    s_send,
    s_recv,
    g_send,
    g_recv,
    own_sem,
    near_sem,
    far_sem,
    row_sem,
    plane_sem,
):
    seq, head = lax.axis_index("seq"), lax.axis_index("head")
    z, x = seq // NX, seq % NX
    y, core = head // NC, head % NC

    def at_z(d):
        other = (z + d) % NZ
        return other, (other * NX + x, head)

    def at_x(d):
        other = (x + d) % NX
        return other, (z * NX + other, head)

    def at_plane(d):
        ox, oy, oc = (x + d[0]) % NX, (y + d[1]) % NY, (core + d[2]) % NC
        return ox * NY + oy, (z * NX + ox, oy * NC + oc)

    def signal(sem, device):
        pl.semaphore_signal(sem, inc=1, device_id=device, device_id_type=MESH)

    def send(src, dst, send_sem, recv_sem, device):
        pltpu.make_async_remote_copy(
            src_ref=src,
            dst_ref=dst,
            send_sem=send_sem,
            recv_sem=recv_sem,
            device_id=device,
            device_id_type=MESH,
        ).start()

    def wait(ref, sem):
        pltpu.make_async_copy(ref, ref, sem).wait()

    loads = []
    for i, (src, dst) in enumerate(
        (
            (k_hbm, raw.at[0]),
            (v_hbm, raw.at[1]),
            (q_hbm, raw.at[2]),
            (t_hbm, raw.at[3]),
            (kmap_hbm, maps.at[0]),
            (qmap_hbm, maps.at[1]),
        )
    ):
        load = pltpu.make_async_copy(src, dst, load_sem.at[i])
        load.start()
        loads.append(load)

    barrier = pltpu.get_barrier_semaphore()
    near = [at_x(d)[1] for d in X_FAR_FIRST]
    near += [at_z(d)[1] for d in (2, NZ - 2, 1, NZ - 1)]
    near += [at_plane((0, d, 0))[1] for d in (2, 1, 3)]
    near += [at_plane((0, 0, 1))[1]]
    for device in near:
        signal(barrier, device)

    def widen(i):
        wide[i] = raw[i].astype(F32)
        for b in range(2):
            for h in range(2):
                stage[i, b * 2 + h] = wide[i, pl.ds(b * 2 * TOK + h, TOK, stride=2), :]
        held[i, x] = stage[i, x]

    def send_x(i):
        for d in X_FAR_FIRST:
            other, device = at_x(d)
            send(stage.at[i, other], held.at[i, x], x_send.at[i], x_recv.at[i], device)

    loads[0].wait()
    widen(0)
    loads[1].wait()
    widen(1)
    pl.semaphore_wait(barrier, len(near))
    send_x(0)
    send_x(1)
    for d in (2, NZ - 2):
        signal(near_sem, at_z(d)[1])
    for d in (2, 1, 3):
        signal(row_sem, at_plane((0, d, 0))[1])
    loads[2].wait()
    widen(2)
    send_x(2)
    loads[3].wait()
    widen(3)
    send_x(3)
    loads[4].wait()
    loads[5].wait()
    pl.semaphore_wait(near_sem, 2)
    for d in (4, NZ - 4):
        signal(far_sem, at_z(d)[1])
    pl.semaphore_wait(row_sem, 3)
    signal(plane_sem, at_plane((0, 0, 1))[1])

    def receive_x(i):
        wait(held.at[i, pl.ds(0, NX - 1)], x_recv.at[i])
        return held[i].reshape(LOC, DH)

    def scatter_z(scan, full_state, full_norm):
        state[scan, :, :FC, :] = full_state.reshape(NZ, FC, DH)
        for i in range(2):
            state[scan, :, FC + i, :] = jnp.broadcast_to(full_norm[:, i * DH : (i + 1) * DH], (NZ, DH))
        for d in Z_FAR_FIRST:
            other, device = at_z(d)
            send(state.at[scan, other], got_state.at[scan, z], z_send.at[2 * scan], z_recv.at[2 * scan], device)
        got_state[scan, z] = state[scan, z]

    def return_z(scan, reverse):
        wait(got_state.at[scan, pl.ds(0, NZ - 1)], z_recv.at[2 * scan])
        order = range(NZ - 1, -1, -1) if reverse else range(NZ)
        running = jnp.zeros((FC, DH), F32)
        for one in order:
            totals[scan, one] = running
            running = running + got_state[scan, one, :FC, :]
        for d in Z_FAR_FIRST:
            other, device = at_z(d)
            send(totals.at[scan, other], entering.at[scan, z], z_send.at[2 * scan + 1], z_recv.at[2 * scan + 1], device)
        entering[scan, z] = totals[scan, z]
        norm = [jnp.zeros((1, DH), F32)] * 2
        for one in order:
            before = one > z if reverse else one < z
            for i in range(2):
                norm[i] = norm[i] + jnp.where(before, got_state[scan, one, FC + i : FC + i + 1, :], 0.0)
        return jnp.concatenate(norm, 1)

    def receive_z(scan):
        wait(entering.at[scan, pl.ds(0, NZ - 1)], z_recv.at[2 * scan + 1])
        return entering[scan].reshape(F2, DH)

    mine = x * NY + y

    def reduce_plane(which, grad):
        part[which] = grad.reshape(NP, 8, DH)
        for d in PLANE_FAR_FIRST:
            other, device = at_plane(d)
            send(part.at[which, other], got_part.at[which, mine * NC + core], r_send.at[which], r_recv.at[which], device)
        got_part[which, mine * NC + core] = part[which, mine]

    def reduce_z(which):
        wait(got_part.at[which, pl.ds(0, NP * NC - 1)], r_recv.at[which])
        sums[which, 0] = jnp.sum(got_part[which], 0)
        for d in Z_FAR_FIRST:
            send(sums.at[which, 0], got_sum.at[which, z], s_send.at[which], s_recv.at[which], at_z(d)[1])
        got_sum[which, z] = sums[which, 0]

    def share(which):
        wait(got_sum.at[which, pl.ds(0, NZ - 1)], s_recv.at[which])
        sums[which, 1] = jnp.sum(got_sum[which], 0)
        for d in PLANE_FAR_FIRST:
            if not d[2]:
                send(sums.at[which, 1], out_ref.at[which, mine], g_send.at[which], g_recv.at[which], at_plane(d)[1])
        pltpu.make_async_copy(sums.at[which, 1], out_ref.at[which, mine], own_sem.at[which]).start()

    keys = receive_x(0).astype(BF16)
    key_phi = feature(keys, maps[0])
    kphi = split(key_phi)
    key_sum = jnp.sum(key_phi, 0, keepdims=True)
    values = receive_x(1).astype(BF16)
    local = mm2(kphi, values, TN)
    pl.semaphore_wait(far_sem, 2)
    scatter_z(0, local, key_sum)

    queries = receive_x(2).astype(BF16)
    query_phi = feature(queries, maps[1])
    qphi = split(query_phi)

    prefix_norm = return_z(0, False)
    causal = lax.broadcasted_iota(jnp.int32, (LOC, LOC), 0) >= lax.broadcasted_iota(
        jnp.int32, (LOC, LOC), 1
    )
    scores = jnp.where(causal, mm3(qphi, kphi, NT), 0.0)
    inner_num = mm2(split(scores), values, NN)
    denominator = jnp.sum(scores, 1, keepdims=True) + jnp.sum(query_phi * prefix_norm, 1, keepdims=True)
    target = receive_x(3)

    prefix = split(receive_z(0))
    output = (inner_num + mm3(qphi, prefix, NN)) / denominator
    misfit = output - target
    grad_num = misfit / denominator
    grad_den = -jnp.sum(misfit * output, 1, keepdims=True) / denominator
    gnum = split(grad_num)
    scatter_z(1, mm3(qphi, gnum, TN), jnp.sum(query_phi * grad_den, 0, keepdims=True))

    mixed = split(jnp.where(causal, mm2(gnum, values, NT) + grad_den, 0.0))
    query_dphi = mm3(mixed, kphi, NN) + mm3(gnum, prefix, NT) + grad_den * prefix_norm
    grad_aq = split(feature_back(query_phi, query_dphi))
    grad_q = mm(queries, grad_aq[0], TN) + mm(queries, grad_aq[1], TN)
    pl.semaphore_wait(plane_sem, 1)
    reduce_plane(0, grad_q)
    key_inner = mm3(mixed, qphi, TN)

    suffix_norm = return_z(1, True)
    reduce_z(0)
    suffix = split(receive_z(1))
    key_dphi = key_inner + mm(values, suffix[0], NT) + mm(values, suffix[1], NT) + suffix_norm
    grad_ak = split(feature_back(key_phi, key_dphi))
    reduce_plane(1, mm(keys, grad_ak[0], TN) + mm(keys, grad_ak[1], TN))
    share(0)
    reduce_z(1)
    share(1)

    for i in range(4):
        wait(held.at[i, pl.ds(0, NX - 1)], x_send.at[i])
    for scan in range(2):
        wait(state.at[scan, pl.ds(0, NZ - 1)], z_send.at[2 * scan])
        wait(totals.at[scan, pl.ds(0, NZ - 1)], z_send.at[2 * scan + 1])
    for which in range(2):
        wait(got_part.at[which, pl.ds(0, NP * NC - 1)], r_send.at[which])
        wait(got_sum.at[which, pl.ds(0, NZ - 1)], s_send.at[which])
        wait(got_part.at[which, pl.ds(0, NP - 1)], g_send.at[which])
        wait(sums.at[which, 1], own_sem.at[which])
        wait(out_ref.at[which, pl.ds(0, NP - 1)], g_recv.at[which])


def per_device(queries, keys, values, teacher, query_map, key_map):
    def flat(a):
        return a.reshape(-1, DH)

    def dma(*shape):
        return pltpu.SemaphoreType.DMA(shape)

    out = pl.pallas_call(
        kernel,
        out_shape=jax.ShapeDtypeStruct((2, NP, 8, DH), F32),
        in_specs=[pl.BlockSpec(memory_space=pl.ANY)] * 6,
        out_specs=pl.BlockSpec(memory_space=pl.ANY),
        scratch_shapes=[
            pltpu.VMEM((4, 4 * TOK, DH), BF16),
            pltpu.VMEM((2, DH, DH), BF16),
            pltpu.VMEM((4, 4 * TOK, DH), F32),
            pltpu.VMEM((4, 4, TOK, DH), F32),
            pltpu.VMEM((4, NX, TOK, DH), F32),
            pltpu.VMEM((2, NZ, ROWS, DH), F32),
            pltpu.VMEM((2, NZ, ROWS, DH), F32),
            pltpu.VMEM((2, NZ, FC, DH), F32),
            pltpu.VMEM((2, NZ, FC, DH), F32),
            pltpu.VMEM((2, NP, 8, DH), F32),
            pltpu.VMEM((2, NP * NC, 8, DH), F32),
            pltpu.VMEM((2, 2, 8, DH), F32),
            pltpu.VMEM((2, NZ, 8, DH), F32),
            dma(6),
            dma(4),
            dma(4),
            dma(4),
            dma(4),
            dma(2),
            dma(2),
            dma(2),
            dma(2),
            dma(2),
            dma(2),
            dma(2),
            pltpu.SemaphoreType.REGULAR,
            pltpu.SemaphoreType.REGULAR,
            pltpu.SemaphoreType.REGULAR,
            pltpu.SemaphoreType.REGULAR,
        ],
        compiler_params=pltpu.CompilerParams(
            collective_id=0, has_side_effects=True, vmem_limit_bytes=56 * 1024 * 1024
        ),
        name="hedgehog",
    )(flat(keys), flat(values), flat(queries), flat(teacher), query_map, key_map)
    return out[0].reshape(DH, DH), out[1].reshape(DH, DH)


def solution(mesh):
    split_spec = P(None, "seq", "head", None)
    return jax.shard_map(
        per_device,
        mesh=mesh,
        in_specs=(split_spec,) * 4 + (P(), P()),
        out_specs=(P(), P()),
        check_vma=False,
    )
```

```python
import jax
import jax.numpy as jnp
from jax import lax
from jax.experimental import pallas as pl
from jax.experimental.pallas import tpu as pltpu
from jax.sharding import PartitionSpec as P

MESH = pl.DeviceIdType.MESH
F32 = jnp.float32
BF16 = jnp.bfloat16

NZ, NX, NY, NC = 16, 4, 4, 2
TOK = 128
DH = 128
F2 = 256
LOC = NX * TOK
FC = F2 // NZ
Z_FAR_FIRST = (8, 7, 9, 6, 10, 5, 11, 4, 12, 3, 13, 2, 14, 1, 15)
X_FAR_FIRST = (2, 1, 3)
PLANE_FAR_FIRST = tuple(
    sorted(
        ((dx, dy, dc) for dx in range(NX) for dy in range(NY) for dc in range(NC) if dx or dy or dc),
        key=lambda d: -(min(d[0], NX - d[0]) + min(d[1], NY - d[1])),
    )
)
NP = NX * NY
ROWS = FC + 2

NN = (((1,), (0,)), ((), ()))
NT = (((1,), (1,)), ((), ()))
TN = (((0,), (0,)), ((), ()))


def split(a):
    high = a.astype(BF16)
    return high, (a - high.astype(F32)).astype(BF16)


def mm(a, b, dims):
    return lax.dot_general(a, b, dims, preferred_element_type=F32)


def mm3(a, b, dims):
    return mm(a[0], b[0], dims) + (mm(a[0], b[1], dims) + mm(a[1], b[0], dims))


def mm2(a, b, dims):
    return mm(a[0], b, dims) + mm(a[1], b, dims)


def feature(inputs, matrix):
    logits = mm(inputs, matrix, NN)
    rising = jnp.exp(logits)
    falling = jnp.exp(-logits)
    return jnp.concatenate(
        [
            rising / jnp.sum(rising, -1, keepdims=True),
            falling / jnp.sum(falling, -1, keepdims=True),
        ],
        -1,
    )


def feature_back(phi, dphi):
    half = phi.shape[-1] // 2
    up, down = phi[:, :half], phi[:, half:]
    grad_up, grad_down = dphi[:, :half], dphi[:, half:]
    return up * (grad_up - jnp.sum(up * grad_up, -1, keepdims=True)) - down * (
        grad_down - jnp.sum(down * grad_down, -1, keepdims=True)
    )


def kernel(
    k_hbm,
    v_hbm,
    q_hbm,
    t_hbm,
    qmap_hbm,
    kmap_hbm,
    out_ref,
    raw,
    maps,
    wide,
    stage,
    held,
    state,
    got_state,
    totals,
    entering,
    part,
    got_part,
    sums,
    got_sum,
    load_sem,
    x_send,
    x_recv,
    z_send,
    z_recv,
    r_send,
    r_recv,
    s_send,
    s_recv,
    g_send,
    g_recv,
    own_sem,
    near_sem,
    far_sem,
    row_sem,
    plane_sem,
):
    seq, head = lax.axis_index("seq"), lax.axis_index("head")
    z, x = seq // NX, seq % NX
    y, core = head // NC, head % NC

    def at_z(d):
        other = (z + d) % NZ
        return other, (other * NX + x, head)

    def at_x(d):
        other = (x + d) % NX
        return other, (z * NX + other, head)

    def at_plane(d):
        ox, oy, oc = (x + d[0]) % NX, (y + d[1]) % NY, (core + d[2]) % NC
        return ox * NY + oy, (z * NX + ox, oy * NC + oc)

    def signal(sem, device):
        pl.semaphore_signal(sem, inc=1, device_id=device, device_id_type=MESH)

    def send(src, dst, send_sem, recv_sem, device):
        pltpu.make_async_remote_copy(
            src_ref=src,
            dst_ref=dst,
            send_sem=send_sem,
            recv_sem=recv_sem,
            device_id=device,
            device_id_type=MESH,
        ).start()

    def wait(ref, sem):
        pltpu.make_async_copy(ref, ref, sem).wait()

    loads = []
    for i, (src, dst) in enumerate(
        (
            (k_hbm, raw.at[0]),
            (v_hbm, raw.at[1]),
            (q_hbm, raw.at[2]),
            (t_hbm, raw.at[3]),
            (kmap_hbm, maps.at[0]),
            (qmap_hbm, maps.at[1]),
        )
    ):
        load = pltpu.make_async_copy(src, dst, load_sem.at[i])
        load.start()
        loads.append(load)

    barrier = pltpu.get_barrier_semaphore()
    near = [at_x(d)[1] for d in X_FAR_FIRST]
    near += [at_z(d)[1] for d in (2, NZ - 2, 1, NZ - 1)]
    near += [at_plane((0, d, 0))[1] for d in (2, 1, 3)]
    near += [at_plane((0, 0, 1))[1]]
    for device in near:
        signal(barrier, device)

    def widen(i):
        wide[i] = raw[i].astype(F32)
        for b in range(2):
            for h in range(2):
                stage[i, b * 2 + h] = wide[i, pl.ds(b * 2 * TOK + h, TOK, stride=2), :]
        held[i, x] = stage[i, x]

    def send_x(i):
        for d in X_FAR_FIRST:
            other, device = at_x(d)
            send(stage.at[i, other], held.at[i, x], x_send.at[i], x_recv.at[i], device)

    loads[0].wait()
    widen(0)
    loads[1].wait()
    widen(1)
    pl.semaphore_wait(barrier, len(near))
    send_x(0)
    send_x(1)
    for d in (2, NZ - 2):
        signal(near_sem, at_z(d)[1])
    for d in (2, 1, 3):
        signal(row_sem, at_plane((0, d, 0))[1])
    loads[2].wait()
    widen(2)
    loads[3].wait()
    widen(3)
    loads[4].wait()
    loads[5].wait()
    pl.semaphore_wait(near_sem, 2)
    for d in (4, NZ - 4):
        signal(far_sem, at_z(d)[1])
    pl.semaphore_wait(row_sem, 3)
    signal(plane_sem, at_plane((0, 0, 1))[1])

    def receive_x(i):
        wait(held.at[i, pl.ds(0, NX - 1)], x_recv.at[i])
        return held[i].reshape(LOC, DH)

    def scatter_z(scan, full_state, full_norm):
        state[scan, :, :FC, :] = full_state.reshape(NZ, FC, DH)
        for i in range(2):
            state[scan, :, FC + i, :] = jnp.broadcast_to(full_norm[:, i * DH : (i + 1) * DH], (NZ, DH))
        for d in Z_FAR_FIRST:
            other, device = at_z(d)
            send(state.at[scan, other], got_state.at[scan, z], z_send.at[2 * scan], z_recv.at[2 * scan], device)
        got_state[scan, z] = state[scan, z]

    def return_z(scan, reverse):
        wait(got_state.at[scan, pl.ds(0, NZ - 1)], z_recv.at[2 * scan])
        order = range(NZ - 1, -1, -1) if reverse else range(NZ)
        running = jnp.zeros((FC, DH), F32)
        for one in order:
            totals[scan, one] = running
            running = running + got_state[scan, one, :FC, :]
        for d in Z_FAR_FIRST:
            other, device = at_z(d)
            send(totals.at[scan, other], entering.at[scan, z], z_send.at[2 * scan + 1], z_recv.at[2 * scan + 1], device)
        entering[scan, z] = totals[scan, z]
        norm = [jnp.zeros((1, DH), F32)] * 2
        for one in order:
            before = one > z if reverse else one < z
            for i in range(2):
                norm[i] = norm[i] + jnp.where(before, got_state[scan, one, FC + i : FC + i + 1, :], 0.0)
        return jnp.concatenate(norm, 1)

    def receive_z(scan):
        wait(entering.at[scan, pl.ds(0, NZ - 1)], z_recv.at[2 * scan + 1])
        return entering[scan].reshape(F2, DH)

    mine = x * NY + y

    def reduce_plane(which, grad):
        part[which] = grad.reshape(NP, 8, DH)
        for d in PLANE_FAR_FIRST:
            other, device = at_plane(d)
            send(part.at[which, other], got_part.at[which, mine * NC + core], r_send.at[which], r_recv.at[which], device)
        got_part[which, mine * NC + core] = part[which, mine]

    def reduce_z(which):
        wait(got_part.at[which, pl.ds(0, NP * NC - 1)], r_recv.at[which])
        sums[which, 0] = jnp.sum(got_part[which], 0)
        for d in Z_FAR_FIRST:
            send(sums.at[which, 0], got_sum.at[which, z], s_send.at[which], s_recv.at[which], at_z(d)[1])
        got_sum[which, z] = sums[which, 0]

    def share(which):
        wait(got_sum.at[which, pl.ds(0, NZ - 1)], s_recv.at[which])
        sums[which, 1] = jnp.sum(got_sum[which], 0)
        for d in PLANE_FAR_FIRST:
            if not d[2]:
                send(sums.at[which, 1], out_ref.at[which, mine], g_send.at[which], g_recv.at[which], at_plane(d)[1])
        pltpu.make_async_copy(sums.at[which, 1], out_ref.at[which, mine], own_sem.at[which]).start()

    keys = receive_x(0).astype(BF16)
    key_phi = feature(keys, maps[0])
    kphi = split(key_phi)
    key_sum = jnp.sum(key_phi, 0, keepdims=True)
    values = receive_x(1).astype(BF16)
    local = mm2(kphi, values, TN)
    pl.semaphore_wait(far_sem, 2)
    scatter_z(0, local, key_sum)
    send_x(2)
    send_x(3)

    queries = receive_x(2).astype(BF16)
    query_phi = feature(queries, maps[1])
    qphi = split(query_phi)

    prefix_norm = return_z(0, False)
    causal = lax.broadcasted_iota(jnp.int32, (LOC, LOC), 0) >= lax.broadcasted_iota(
        jnp.int32, (LOC, LOC), 1
    )
    scores = jnp.where(causal, mm3(qphi, kphi, NT), 0.0)
    inner_num = mm2(split(scores), values, NN)
    denominator = jnp.sum(scores, 1, keepdims=True) + jnp.sum(query_phi * prefix_norm, 1, keepdims=True)
    target = receive_x(3)

    prefix = split(receive_z(0))
    output = (inner_num + mm3(qphi, prefix, NN)) / denominator
    misfit = output - target
    grad_num = misfit / denominator
    grad_den = -jnp.sum(misfit * output, 1, keepdims=True) / denominator
    gnum = split(grad_num)
    scatter_z(1, mm3(qphi, gnum, TN), jnp.sum(query_phi * grad_den, 0, keepdims=True))

    mixed = split(jnp.where(causal, mm2(gnum, values, NT) + grad_den, 0.0))
    query_dphi = mm3(mixed, kphi, NN) + mm3(gnum, prefix, NT) + grad_den * prefix_norm
    grad_aq = split(feature_back(query_phi, query_dphi))
    grad_q = mm(queries, grad_aq[0], TN) + mm(queries, grad_aq[1], TN)
    pl.semaphore_wait(plane_sem, 1)
    reduce_plane(0, grad_q)
    key_inner = mm3(mixed, qphi, TN)

    suffix_norm = return_z(1, True)
    reduce_z(0)
    suffix = split(receive_z(1))
    key_dphi = key_inner + mm(values, suffix[0], NT) + mm(values, suffix[1], NT) + suffix_norm
    grad_ak = split(feature_back(key_phi, key_dphi))
    reduce_plane(1, mm(keys, grad_ak[0], TN) + mm(keys, grad_ak[1], TN))
    share(0)
    reduce_z(1)
    share(1)

    for i in range(4):
        wait(held.at[i, pl.ds(0, NX - 1)], x_send.at[i])
    for scan in range(2):
        wait(state.at[scan, pl.ds(0, NZ - 1)], z_send.at[2 * scan])
        wait(totals.at[scan, pl.ds(0, NZ - 1)], z_send.at[2 * scan + 1])
    for which in range(2):
        wait(got_part.at[which, pl.ds(0, NP * NC - 1)], r_send.at[which])
        wait(got_sum.at[which, pl.ds(0, NZ - 1)], s_send.at[which])
        wait(got_part.at[which, pl.ds(0, NP - 1)], g_send.at[which])
        wait(sums.at[which, 1], own_sem.at[which])
        wait(out_ref.at[which, pl.ds(0, NP - 1)], g_recv.at[which])


def per_device(queries, keys, values, teacher, query_map, key_map):
    def flat(a):
        return a.reshape(-1, DH)

    def dma(*shape):
        return pltpu.SemaphoreType.DMA(shape)

    out = pl.pallas_call(
        kernel,
        out_shape=jax.ShapeDtypeStruct((2, NP, 8, DH), F32),
        in_specs=[pl.BlockSpec(memory_space=pl.ANY)] * 6,
        out_specs=pl.BlockSpec(memory_space=pl.ANY),
        scratch_shapes=[
            pltpu.VMEM((4, 4 * TOK, DH), BF16),
            pltpu.VMEM((2, DH, DH), BF16),
            pltpu.VMEM((4, 4 * TOK, DH), F32),
            pltpu.VMEM((4, 4, TOK, DH), F32),
            pltpu.VMEM((4, NX, TOK, DH), F32),
            pltpu.VMEM((2, NZ, ROWS, DH), F32),
            pltpu.VMEM((2, NZ, ROWS, DH), F32),
            pltpu.VMEM((2, NZ, FC, DH), F32),
            pltpu.VMEM((2, NZ, FC, DH), F32),
            pltpu.VMEM((2, NP, 8, DH), F32),
            pltpu.VMEM((2, NP * NC, 8, DH), F32),
            pltpu.VMEM((2, 2, 8, DH), F32),
            pltpu.VMEM((2, NZ, 8, DH), F32),
            dma(6),
            dma(4),
            dma(4),
            dma(4),
            dma(4),
            dma(2),
            dma(2),
            dma(2),
            dma(2),
            dma(2),
            dma(2),
            dma(2),
            pltpu.SemaphoreType.REGULAR,
            pltpu.SemaphoreType.REGULAR,
            pltpu.SemaphoreType.REGULAR,
            pltpu.SemaphoreType.REGULAR,
        ],
        compiler_params=pltpu.CompilerParams(
            collective_id=0, has_side_effects=True, vmem_limit_bytes=56 * 1024 * 1024
        ),
        name="hedgehog",
    )(flat(keys), flat(values), flat(queries), flat(teacher), query_map, key_map)
    return out[0].reshape(DH, DH), out[1].reshape(DH, DH)


def solution(mesh):
    split_spec = P(None, "seq", "head", None)
    return jax.shard_map(
        per_device,
        mesh=mesh,
        in_specs=(split_spec,) * 4 + (P(), P()),
        out_specs=(P(), P()),
        check_vma=False,
    )
```

```python
import jax
import jax.numpy as jnp
from jax import lax
from jax.experimental import pallas as pl
from jax.experimental.pallas import tpu as pltpu
from jax.sharding import PartitionSpec as P

MESH = pl.DeviceIdType.MESH
F32 = jnp.float32
BF16 = jnp.bfloat16

NZ, NX, NY, NC = 16, 4, 4, 2
TOK = 128
DH = 128
F2 = 256
LOC = NX * TOK
FC = DH // NZ
Z_FAR_FIRST = (8, 7, 9, 6, 10, 5, 11, 4, 12, 3, 13, 2, 14, 1, 15)
X_FAR_FIRST = (2, 1, 3)
PLANE_FAR_FIRST = tuple(
    sorted(
        ((dx, dy, dc) for dx in range(NX) for dy in range(NY) for dc in range(NC) if dx or dy or dc),
        key=lambda d: -(min(d[0], NX - d[0]) + min(d[1], NY - d[1])),
    )
)
NP = NX * NY
ROWS = FC + 1

NN = (((1,), (0,)), ((), ()))
NT = (((1,), (1,)), ((), ()))
TN = (((0,), (0,)), ((), ()))


def split(a):
    high = a.astype(BF16)
    return high, (a - high.astype(F32)).astype(BF16)


def mm(a, b, dims):
    return lax.dot_general(a, b, dims, preferred_element_type=F32)


def mm3(a, b, dims):
    return mm(a[0], b[0], dims) + (mm(a[0], b[1], dims) + mm(a[1], b[0], dims))


def mm2(a, b, dims):
    return mm(a[0], b, dims) + mm(a[1], b, dims)


def feature(inputs, matrix):
    logits = mm(inputs, matrix, NN)
    rising = jnp.exp(logits)
    falling = jnp.exp(-logits)
    return jnp.concatenate(
        [
            rising / jnp.sum(rising, -1, keepdims=True),
            falling / jnp.sum(falling, -1, keepdims=True),
        ],
        -1,
    )


def feature_back(phi, dphi):
    return phi * (dphi - jnp.sum(phi * dphi, -1, keepdims=True))


def kernel(
    k_hbm,
    v_hbm,
    q_hbm,
    t_hbm,
    qmap_hbm,
    kmap_hbm,
    out_ref,
    raw,
    maps,
    wide,
    stage,
    held,
    state,
    got_state,
    totals,
    entering,
    part,
    got_part,
    sums,
    got_sum,
    load_sem,
    x_send,
    x_recv,
    z_send,
    z_recv,
    r_send,
    r_recv,
    s_send,
    s_recv,
    g_send,
    g_recv,
    own_sem,
    near_sem,
    far_sem,
    row_sem,
    plane_sem,
):
    seq, head = lax.axis_index("seq"), lax.axis_index("head")
    z, x = seq // NX, seq % NX
    y, core = head // NC, head % NC

    def at_z(d):
        other = (z + d) % NZ
        return other, (other * NX + x, head)

    def at_x(d):
        other = (x + d) % NX
        return other, (z * NX + other, head)

    def at_plane(d):
        ox, oy, oc = (x + d[0]) % NX, (y + d[1]) % NY, (core + d[2]) % NC
        return ox * NY + oy, (z * NX + ox, oy * NC + oc)

    def signal(sem, device):
        pl.semaphore_signal(sem, inc=1, device_id=device, device_id_type=MESH)

    def send(src, dst, send_sem, recv_sem, device):
        pltpu.make_async_remote_copy(
            src_ref=src,
            dst_ref=dst,
            send_sem=send_sem,
            recv_sem=recv_sem,
            device_id=device,
            device_id_type=MESH,
        ).start()

    def wait(ref, sem):
        pltpu.make_async_copy(ref, ref, sem).wait()

    loads = []
    for i, (src, dst) in enumerate(
        (
            (k_hbm, raw.at[0]),
            (v_hbm, raw.at[1]),
            (q_hbm, raw.at[2]),
            (t_hbm, raw.at[3]),
            (kmap_hbm, maps.at[0]),
            (qmap_hbm, maps.at[1]),
        )
    ):
        load = pltpu.make_async_copy(src, dst, load_sem.at[i])
        load.start()
        loads.append(load)

    barrier = pltpu.get_barrier_semaphore()
    near = [at_x(d)[1] for d in X_FAR_FIRST]
    near += [at_z(d)[1] for d in (2, NZ - 2, 1, NZ - 1)]
    near += [at_plane((0, d, 0))[1] for d in (2, 1, 3)]
    near += [at_plane((0, 0, 1))[1]]
    for device in near:
        signal(barrier, device)

    def widen(i):
        wide[i] = raw[i].astype(F32)
        for b in range(2):
            for h in range(2):
                stage[i, b * 2 + h] = wide[i, pl.ds(b * 2 * TOK + h, TOK, stride=2), :]
        held[i, x] = stage[i, x]

    def send_x(i):
        for d in X_FAR_FIRST:
            other, device = at_x(d)
            send(stage.at[i, other], held.at[i, x], x_send.at[i], x_recv.at[i], device)

    loads[0].wait()
    widen(0)
    loads[1].wait()
    widen(1)
    pl.semaphore_wait(barrier, len(near))
    send_x(0)
    send_x(1)
    for d in (2, NZ - 2):
        signal(near_sem, at_z(d)[1])
    for d in (2, 1, 3):
        signal(row_sem, at_plane((0, d, 0))[1])
    loads[2].wait()
    widen(2)
    loads[3].wait()
    widen(3)
    loads[4].wait()
    loads[5].wait()
    pl.semaphore_wait(near_sem, 2)
    for d in (4, NZ - 4):
        signal(far_sem, at_z(d)[1])
    pl.semaphore_wait(row_sem, 3)
    signal(plane_sem, at_plane((0, 0, 1))[1])

    def receive_x(i):
        wait(held.at[i, pl.ds(0, NX - 1)], x_recv.at[i])
        return held[i].reshape(LOC, DH)

    def scatter_z(scan, sign, rows, norm):
        state[scan, sign, :, :FC, :] = rows.reshape(NZ, FC, DH)
        state[scan, sign, :, FC, :] = jnp.broadcast_to(norm, (NZ, DH))
        sem = 4 * scan + sign
        for d in Z_FAR_FIRST:
            other, device = at_z(d)
            send(state.at[scan, sign, other], got_state.at[scan, sign, z], z_send.at[sem], z_recv.at[sem], device)
        got_state[scan, sign, z] = state[scan, sign, z]

    def return_z(scan, sign, reverse):
        sem = 4 * scan + sign
        wait(got_state.at[scan, sign, pl.ds(0, NZ - 1)], z_recv.at[sem])
        order = range(NZ - 1, -1, -1) if reverse else range(NZ)
        running = jnp.zeros((FC, DH), F32)
        for one in order:
            totals[scan, sign, one] = running
            running = running + got_state[scan, sign, one, :FC, :]
        for d in Z_FAR_FIRST:
            other, device = at_z(d)
            send(totals.at[scan, sign, other], entering.at[scan, sign, z], z_send.at[sem + 2], z_recv.at[sem + 2], device)
        entering[scan, sign, z] = totals[scan, sign, z]

    def norm_z(scan, sign, reverse):
        norm = jnp.zeros((1, DH), F32)
        for one in range(NZ):
            before = one > z if reverse else one < z
            norm = norm + jnp.where(before, got_state[scan, sign, one, FC : FC + 1, :], 0.0)
        return norm

    def receive_z(scan, sign):
        wait(entering.at[scan, sign, pl.ds(0, NZ - 1)], z_recv.at[4 * scan + sign + 2])
        return entering[scan, sign].reshape(DH, DH)

    mine = x * NY + y

    def reduce_plane(which, grad):
        part[which] = grad.reshape(NP, 8, DH)
        for d in PLANE_FAR_FIRST:
            other, device = at_plane(d)
            send(part.at[which, other], got_part.at[which, mine * NC + core], r_send.at[which], r_recv.at[which], device)
        got_part[which, mine * NC + core] = part[which, mine]

    def reduce_z(which):
        wait(got_part.at[which, pl.ds(0, NP * NC - 1)], r_recv.at[which])
        sums[which, 0] = jnp.sum(got_part[which], 0)
        for d in Z_FAR_FIRST:
            send(sums.at[which, 0], got_sum.at[which, z], s_send.at[which], s_recv.at[which], at_z(d)[1])
        got_sum[which, z] = sums[which, 0]

    def share(which):
        wait(got_sum.at[which, pl.ds(0, NZ - 1)], s_recv.at[which])
        sums[which, 1] = jnp.sum(got_sum[which], 0)
        for d in PLANE_FAR_FIRST:
            if not d[2]:
                send(sums.at[which, 1], out_ref.at[which, mine], g_send.at[which], g_recv.at[which], at_plane(d)[1])
        pltpu.make_async_copy(sums.at[which, 1], out_ref.at[which, mine], own_sem.at[which]).start()

    def of(sign, pair):
        return tuple(a[:, sign * DH : (sign + 1) * DH] for a in pair)

    keys = receive_x(0).astype(BF16)
    key_phi = feature(keys, maps[0])
    kphi = split(key_phi)
    key_sum = jnp.sum(key_phi, 0, keepdims=True)
    values = receive_x(1).astype(BF16)
    for sign in range(2):
        local = mm2(of(sign, kphi), values, TN)
        if sign == 0:
            pl.semaphore_wait(far_sem, 2)
        scatter_z(0, sign, local, key_sum[:, sign * DH : (sign + 1) * DH])
    send_x(2)
    send_x(3)

    queries = receive_x(2).astype(BF16)
    query_phi = feature(queries, maps[1])
    qphi = split(query_phi)

    for sign in range(2):
        return_z(0, sign, False)
    prefix_norm = jnp.concatenate([norm_z(0, sign, False) for sign in range(2)], 1)
    causal = lax.broadcasted_iota(jnp.int32, (LOC, LOC), 0) >= lax.broadcasted_iota(
        jnp.int32, (LOC, LOC), 1
    )
    scores = jnp.where(causal, mm3(qphi, kphi, NT), 0.0)
    numerator = mm2(split(scores), values, NN)
    denominator = jnp.sum(scores, 1, keepdims=True) + jnp.sum(query_phi * prefix_norm, 1, keepdims=True)
    target = receive_x(3)

    prefix = []
    for sign in range(2):
        prefix.append(split(receive_z(0, sign)))
        numerator = numerator + mm3(of(sign, qphi), prefix[sign], NN)
    output = numerator / denominator
    misfit = output - target
    grad_num = misfit / denominator
    grad_den = -jnp.sum(misfit * output, 1, keepdims=True) / denominator
    gnum = split(grad_num)
    query_sum = jnp.sum(query_phi * grad_den, 0, keepdims=True)
    for sign in range(2):
        scatter_z(1, sign, mm3(of(sign, qphi), gnum, TN), query_sum[:, sign * DH : (sign + 1) * DH])

    mixed = split(jnp.where(causal, mm2(gnum, values, NT) + grad_den, 0.0))
    query_dphi = (
        mm3(mixed, kphi, NN)
        + jnp.concatenate([mm3(gnum, prefix[sign], NT) for sign in range(2)], 1)
        + grad_den * prefix_norm
    )
    grad_aq = split(
        feature_back(query_phi[:, :DH], query_dphi[:, :DH]) - feature_back(query_phi[:, DH:], query_dphi[:, DH:])
    )
    grad_q = mm(queries, grad_aq[0], TN) + mm(queries, grad_aq[1], TN)
    pl.semaphore_wait(plane_sem, 1)
    reduce_plane(0, grad_q)
    key_inner = mm3(mixed, qphi, TN)

    for sign in range(2):
        return_z(1, sign, True)
    suffix_norm = jnp.concatenate([norm_z(1, sign, True) for sign in range(2)], 1)
    key_inner = key_inner + suffix_norm
    reduce_z(0)
    grad_ak = []
    for sign in range(2):
        suffix = split(receive_z(1, sign))
        lanes = slice(sign * DH, (sign + 1) * DH)
        key_dphi = key_inner[:, lanes] + mm(values, suffix[0], NT) + mm(values, suffix[1], NT)
        grad_ak.append(feature_back(key_phi[:, lanes], key_dphi))
    grad_ak = split(grad_ak[0] - grad_ak[1])
    reduce_plane(1, mm(keys, grad_ak[0], TN) + mm(keys, grad_ak[1], TN))
    share(0)
    reduce_z(1)
    share(1)

    for i in range(4):
        wait(held.at[i, pl.ds(0, NX - 1)], x_send.at[i])
    for scan in range(2):
        for sign in range(2):
            wait(state.at[scan, sign, pl.ds(0, NZ - 1)], z_send.at[4 * scan + sign])
            wait(totals.at[scan, sign, pl.ds(0, NZ - 1)], z_send.at[4 * scan + sign + 2])
    for which in range(2):
        wait(got_part.at[which, pl.ds(0, NP * NC - 1)], r_send.at[which])
        wait(got_sum.at[which, pl.ds(0, NZ - 1)], s_send.at[which])
        wait(got_part.at[which, pl.ds(0, NP - 1)], g_send.at[which])
        wait(sums.at[which, 1], own_sem.at[which])
        wait(out_ref.at[which, pl.ds(0, NP - 1)], g_recv.at[which])


def per_device(queries, keys, values, teacher, query_map, key_map):
    def flat(a):
        return a.reshape(-1, DH)

    def dma(*shape):
        return pltpu.SemaphoreType.DMA(shape)

    out = pl.pallas_call(
        kernel,
        out_shape=jax.ShapeDtypeStruct((2, NP, 8, DH), F32),
        in_specs=[pl.BlockSpec(memory_space=pl.ANY)] * 6,
        out_specs=pl.BlockSpec(memory_space=pl.ANY),
        scratch_shapes=[
            pltpu.VMEM((4, 4 * TOK, DH), BF16),
            pltpu.VMEM((2, DH, DH), BF16),
            pltpu.VMEM((4, 4 * TOK, DH), F32),
            pltpu.VMEM((4, 4, TOK, DH), F32),
            pltpu.VMEM((4, NX, TOK, DH), F32),
            pltpu.VMEM((2, 2, NZ, ROWS, DH), F32),
            pltpu.VMEM((2, 2, NZ, ROWS, DH), F32),
            pltpu.VMEM((2, 2, NZ, FC, DH), F32),
            pltpu.VMEM((2, 2, NZ, FC, DH), F32),
            pltpu.VMEM((2, NP, 8, DH), F32),
            pltpu.VMEM((2, NP * NC, 8, DH), F32),
            pltpu.VMEM((2, 2, 8, DH), F32),
            pltpu.VMEM((2, NZ, 8, DH), F32),
            dma(6),
            dma(4),
            dma(4),
            dma(8),
            dma(8),
            dma(2),
            dma(2),
            dma(2),
            dma(2),
            dma(2),
            dma(2),
            dma(2),
            pltpu.SemaphoreType.REGULAR,
            pltpu.SemaphoreType.REGULAR,
            pltpu.SemaphoreType.REGULAR,
            pltpu.SemaphoreType.REGULAR,
        ],
        compiler_params=pltpu.CompilerParams(
            collective_id=0, has_side_effects=True, vmem_limit_bytes=56 * 1024 * 1024
        ),
        name="hedgehog",
    )(flat(keys), flat(values), flat(queries), flat(teacher), query_map, key_map)
    return out[0].reshape(DH, DH), out[1].reshape(DH, DH)


def solution(mesh):
    split_spec = P(None, "seq", "head", None)
    return jax.shard_map(
        per_device,
        mesh=mesh,
        in_specs=(split_spec,) * 4 + (P(), P()),
        out_specs=(P(), P()),
        check_vma=False,
    )
```

```python
import jax
import jax.numpy as jnp
from jax import lax
from jax.experimental import pallas as pl
from jax.experimental.pallas import tpu as pltpu
from jax.sharding import PartitionSpec as P

MESH = pl.DeviceIdType.MESH
F32 = jnp.float32
BF16 = jnp.bfloat16

NZ, NX, NY, NC = 16, 4, 4, 2
TOK = 128
DH = 128
F2 = 256
LOC = NX * TOK
FC = DH // NZ
Z_FAR = (8, 7, 9, 6, 10, 5, 11)
Z_NEAR = (4, 12, 3, 13, 2, 14, 1, 15)
Z_FAR_FIRST = Z_FAR + Z_NEAR
X_FAR_FIRST = (2, 1, 3)
PLANE_FAR_FIRST = tuple(
    sorted(
        ((dx, dy, dc) for dx in range(NX) for dy in range(NY) for dc in range(NC) if dx or dy or dc),
        key=lambda d: -(min(d[0], NX - d[0]) + min(d[1], NY - d[1])),
    )
)
NP = NX * NY
HALF = DH // 2

NN = (((1,), (0,)), ((), ()))
NT = (((1,), (1,)), ((), ()))
TN = (((0,), (0,)), ((), ()))


def split(a):
    high = a.astype(BF16)
    return high, (a - high.astype(F32)).astype(BF16)


def mm(a, b, dims):
    return lax.dot_general(a, b, dims, preferred_element_type=F32)


def mm3(a, b, dims):
    return mm(a[0], b[0], dims) + (mm(a[0], b[1], dims) + mm(a[1], b[0], dims))


def mm2(a, b, dims):
    return mm(a[0], b, dims) + mm(a[1], b, dims)


def mm_wide(a, b):
    both = mm(a, b, NN)
    return both[:, :DH] + both[:, DH:]


def side(pair):
    return jnp.concatenate(pair, 1)


def feature(inputs, matrix):
    logits = mm(inputs, matrix, NN)
    rising = jnp.exp(logits)
    falling = jnp.exp(-logits)
    return jnp.concatenate(
        [
            rising / jnp.sum(rising, -1, keepdims=True),
            falling / jnp.sum(falling, -1, keepdims=True),
        ],
        -1,
    )


def feature_back(phi, dphi):
    return phi * (dphi - jnp.sum(phi * dphi, -1, keepdims=True))


def kernel(
    k_hbm,
    v_hbm,
    q_hbm,
    t_hbm,
    qmap_hbm,
    kmap_hbm,
    out_ref,
    raw,
    maps,
    wide,
    stage,
    held,
    stage_v,
    held_v,
    state_a,
    got_state_a,
    state_b,
    got_state_b,
    state_c,
    got_state_c,
    totals,
    entering,
    part,
    got_part,
    sums,
    got_sum,
    load_sem,
    x_send,
    x_recv,
    z_send,
    z_recv,
    r_send,
    r_recv,
    s_send,
    s_recv,
    g_send,
    g_recv,
    own_sem,
    near_sem,
    far_sem,
    row_sem,
    plane_sem,
):
    seq, head = lax.axis_index("seq"), lax.axis_index("head")
    z, x = seq // NX, seq % NX
    y, core = head // NC, head % NC

    def at_z(d):
        other = (z + d) % NZ
        return other, (other * NX + x, head)

    def at_x(d):
        other = (x + d) % NX
        return other, (z * NX + other, head)

    def at_plane(d):
        ox, oy, oc = (x + d[0]) % NX, (y + d[1]) % NY, (core + d[2]) % NC
        return ox * NY + oy, (z * NX + ox, oy * NC + oc)

    def signal(sem, device):
        pl.semaphore_signal(sem, inc=1, device_id=device, device_id_type=MESH)

    def send(src, dst, send_sem, recv_sem, device):
        pltpu.make_async_remote_copy(
            src_ref=src,
            dst_ref=dst,
            send_sem=send_sem,
            recv_sem=recv_sem,
            device_id=device,
            device_id_type=MESH,
        ).start()

    def wait(ref, sem):
        pltpu.make_async_copy(ref, ref, sem).wait()

    barrier = pltpu.get_barrier_semaphore()
    near = [at_x(d)[1] for d in X_FAR_FIRST]
    near += [at_z(d)[1] for d in (2, NZ - 2, 1, NZ - 1)]
    near += [at_plane((0, d, 0))[1] for d in (2, 1, 3)]
    near += [at_plane((0, 0, 1))[1]]
    for device in near:
        signal(barrier, device)

    loads = []
    for i, (src, dst) in enumerate(
        (
            (k_hbm, raw.at[0]),
            (v_hbm, raw.at[1]),
            (q_hbm, raw.at[2]),
            (t_hbm, raw.at[3]),
            (kmap_hbm, maps.at[0]),
            (qmap_hbm, maps.at[1]),
        )
    ):
        load = pltpu.make_async_copy(src, dst, load_sem.at[i])
        load.start()
        loads.append(load)

    def widen(i, source):
        wide[source] = raw[source].astype(F32)
        for b in range(2):
            for h in range(2):
                stage[i, b * 2 + h] = wide[source, pl.ds(b * 2 * TOK + h, TOK, stride=2), :]
        held[i, x] = stage[i, x]

    def widen_v():
        wide[1] = raw[1].astype(F32)
        for b in range(2):
            for h in range(2):
                turned = wide[1, pl.ds(b * 2 * TOK + h, TOK, stride=2), :].T
                for half in range(2):
                    stage_v[half, b * 2 + h] = turned[half * HALF : (half + 1) * HALF]
        for half in range(2):
            held_v[half, x] = stage_v[half, x]

    def send_x(i):
        for d in X_FAR_FIRST:
            other, device = at_x(d)
            send(stage.at[i, other], held.at[i, x], x_send.at[i], x_recv.at[i], device)

    def send_v(half):
        for d in X_FAR_FIRST:
            other, device = at_x(d)
            send(stage_v.at[half, other], held_v.at[half, x], x_send.at[3 + half], x_recv.at[3 + half], device)

    loads[0].wait()
    widen(0, 0)
    loads[1].wait()
    widen_v()
    pl.semaphore_wait(barrier, len(near))
    send_x(0)
    send_v(0)
    send_v(1)
    for d in (2, NZ - 2):
        signal(near_sem, at_z(d)[1])
    for d in (2, 1, 3):
        signal(row_sem, at_plane((0, d, 0))[1])
    loads[2].wait()
    widen(1, 2)
    loads[3].wait()
    widen(2, 3)
    loads[4].wait()
    loads[5].wait()
    pl.semaphore_wait(near_sem, 2)
    for d in (4, NZ - 4):
        signal(far_sem, at_z(d)[1])
    pl.semaphore_wait(row_sem, 3)
    signal(plane_sem, at_plane((0, 0, 1))[1])

    def receive_x(i):
        wait(held.at[i, pl.ds(0, NX - 1)], x_recv.at[i])
        return held[i].reshape(LOC, DH)

    def receive_v(half):
        wait(held_v.at[half, pl.ds(0, NX - 1)], x_recv.at[3 + half])
        return jnp.concatenate([held_v[half, i] for i in range(NX)], 1).astype(BF16)

    streams = (
        ((state_a, got_state_a), (state_b, got_state_b)),
        tuple((state_c.at[sign], got_state_c.at[sign]) for sign in range(2)),
    )

    def scatter_z(scan, stream):
        rows, got = streams[scan][stream]
        got[z] = rows[z]
        send_rows(scan, stream, Z_FAR)

    def send_rows(scan, stream, distances):
        rows, got = streams[scan][stream]
        sem = 4 * scan + stream
        for d in distances:
            other, device = at_z(d)
            send(rows.at[other], got.at[z], z_send.at[sem], z_recv.at[sem], device)

    def return_z(scan, stream, reverse):
        got = streams[scan][stream][1]
        sem = 4 * scan + stream
        wait(got.at[pl.ds(0, NZ - 1)], z_recv.at[sem])
        order = range(NZ - 1, -1, -1) if reverse else range(NZ)
        running = jnp.zeros((FC, DH), F32)
        for one in order:
            totals[scan, stream, one] = running
            running = running + got[one, :FC, :]
        entering[scan, stream, z] = totals[scan, stream, z]
        send_totals(scan, stream, Z_FAR)

    def send_totals(scan, stream, distances):
        sem = 4 * scan + stream + 2
        for d in distances:
            other, device = at_z(d)
            send(totals.at[scan, stream, other], entering.at[scan, stream, z], z_send.at[sem], z_recv.at[sem], device)

    def norm_z(got, row, reverse):
        norm = jnp.zeros((1, DH), F32)
        for one in range(NZ):
            before = one > z if reverse else one < z
            norm = norm + jnp.where(before, got[one, row : row + 1, :], 0.0)
        return norm

    def receive_z(scan, stream):
        wait(entering.at[scan, stream, pl.ds(0, NZ - 1)], z_recv.at[4 * scan + stream + 2])
        return entering[scan, stream]

    mine = x * NY + y

    def reduce_plane(which, grad):
        if which == 0:
            pl.semaphore_wait(plane_sem, 1)
        part[which] = grad.reshape(NP, 8, DH)
        for d in PLANE_FAR_FIRST:
            other, device = at_plane(d)
            send(part.at[which, other], got_part.at[which, mine * NC + core], r_send.at[which], r_recv.at[which], device)
        got_part[which, mine * NC + core] = part[which, mine]

    def reduce_z(which):
        wait(got_part.at[which, pl.ds(0, NP * NC - 1)], r_recv.at[which])
        sums[which, 0] = jnp.sum(got_part[which], 0)
        for d in Z_FAR_FIRST:
            send(sums.at[which, 0], got_sum.at[which, z], s_send.at[which], s_recv.at[which], at_z(d)[1])
        got_sum[which, z] = sums[which, 0]

    def share(which):
        wait(got_sum.at[which, pl.ds(0, NZ - 1)], s_recv.at[which])
        sums[which, 1] = jnp.sum(got_sum[which], 0)
        for d in PLANE_FAR_FIRST:
            if not d[2]:
                send(sums.at[which, 1], out_ref.at[which, mine], g_send.at[which], g_recv.at[which], at_plane(d)[1])
        pltpu.make_async_copy(sums.at[which, 1], out_ref.at[which, mine], own_sem.at[which]).start()

    keys = receive_x(0).astype(BF16)
    key_phi = feature(keys, maps[0])
    kphi = split(key_phi)
    key_sum = jnp.sum(key_phi, 0, keepdims=True)
    for i in range(2):
        state_a[:, FC + i, :] = jnp.broadcast_to(key_sum[:, i * DH : (i + 1) * DH], (NZ, DH))
    values_t = []
    for half in range(2):
        values_t.append(receive_v(half))
        local = mm(values_t[half], kphi[0], NN) + mm(values_t[half], kphi[1], NN)
        rows = streams[0][half][0]
        for owner in range(NZ):
            i, j = owner // 2, owner % 2
            rows[owner, :FC, :] = local[i * FC : (i + 1) * FC, j * DH : (j + 1) * DH]
        if half == 0:
            pl.semaphore_wait(far_sem, 2)
        scatter_z(0, half)
    for half in range(2):
        send_rows(0, half, Z_NEAR)
    send_x(1)
    send_x(2)
    values_t = jnp.concatenate(values_t, 0)
    values = values_t.T

    queries = receive_x(1).astype(BF16)
    query_phi = feature(queries, maps[1])
    qphi = split(query_phi)

    for half in range(2):
        return_z(0, half, False)
    for half in range(2):
        send_totals(0, half, Z_NEAR)
    prefix_norm = side([norm_z(got_state_a, FC + i, False) for i in range(2)])
    causal = lax.broadcasted_iota(jnp.int32, (LOC, LOC), 0) >= lax.broadcasted_iota(
        jnp.int32, (LOC, LOC), 1
    )
    scores = jnp.where(causal, mm3(qphi, kphi, NT), 0.0)
    inner_num = mm2(split(scores), values, NN)
    denominator = jnp.sum(scores, 1, keepdims=True) + jnp.sum(query_phi * prefix_norm, 1, keepdims=True)
    target = receive_x(2)
    qphi_t = tuple(a.T for a in qphi)
    keys_t = keys.T

    prefix = []
    for half in range(2):
        blocks = receive_z(0, half)
        for i in range(NZ // 2):
            prefix.append(side([blocks[2 * i], blocks[2 * i + 1]]))
    prefix = split(jnp.concatenate(prefix, 0))
    both = mm(qphi[0], jnp.concatenate(prefix, 0), NT)
    numerator = inner_num + (both[:, :DH] + (both[:, DH:] + mm(qphi[1], prefix[0], NT)))
    output = numerator / denominator
    misfit = output - target
    grad_num = misfit / denominator
    grad_den = -jnp.sum(misfit * output, 1, keepdims=True) / denominator
    gnum = split(grad_num)
    gnum_side = side(gnum)
    query_sum = jnp.sum(query_phi * grad_den, 0, keepdims=True)
    for sign in range(2):
        lanes = slice(sign * DH, (sign + 1) * DH)
        back = mm_wide(qphi_t[0][lanes], gnum_side) + mm(qphi_t[1][lanes], gnum[0], NN)
        state_c[sign, :, :FC, :] = back.reshape(NZ, FC, DH)
        state_c[sign, :, FC, :] = jnp.broadcast_to(query_sum[:, lanes], (NZ, DH))
        scatter_z(1, sign)
    for sign in range(2):
        send_rows(1, sign, Z_NEAR)

    mixed = split(jnp.where(causal, mm2(gnum, values, NT) + grad_den, 0.0))
    query_dphi = mm3(mixed, kphi, NN) + mm3(gnum, prefix, NN) + grad_den * prefix_norm
    grad_aq = split(
        feature_back(query_phi[:, :DH], query_dphi[:, :DH]) - feature_back(query_phi[:, DH:], query_dphi[:, DH:])
    )
    reduce_plane(0, mm_wide(queries.T, side(grad_aq)))
    key_inner = mm3(mixed, qphi, TN)

    for sign in range(2):
        return_z(1, sign, True)
    for sign in range(2):
        send_totals(1, sign, Z_NEAR)
    suffix_norm = side([norm_z(got_state_c.at[sign], FC, True) for sign in range(2)])
    key_inner = key_inner + suffix_norm
    reduce_z(0)
    grad_ak = []
    for sign in range(2):
        suffix = split(receive_z(1, sign).reshape(DH, DH))
        lanes = slice(sign * DH, (sign + 1) * DH)
        both = mm(values, jnp.concatenate(suffix, 0), NT)
        grad_ak.append(feature_back(key_phi[:, lanes], key_inner[:, lanes] + (both[:, :DH] + both[:, DH:])))
    reduce_plane(1, mm_wide(keys_t, side(split(grad_ak[0] - grad_ak[1]))))
    share(0)
    reduce_z(1)
    share(1)

    for i in range(3):
        wait(held.at[i, pl.ds(0, NX - 1)], x_send.at[i])
    for half in range(2):
        wait(held_v.at[half, pl.ds(0, NX - 1)], x_send.at[3 + half])
    for scan in range(2):
        for stream in range(2):
            rows = streams[scan][stream][0]
            wait(rows.at[pl.ds(0, NZ - 1)], z_send.at[4 * scan + stream])
            wait(totals.at[scan, stream, pl.ds(0, NZ - 1)], z_send.at[4 * scan + stream + 2])
    for which in range(2):
        wait(got_part.at[which, pl.ds(0, NP * NC - 1)], r_send.at[which])
        wait(got_sum.at[which, pl.ds(0, NZ - 1)], s_send.at[which])
        wait(got_part.at[which, pl.ds(0, NP - 1)], g_send.at[which])
        wait(sums.at[which, 1], own_sem.at[which])
        wait(out_ref.at[which, pl.ds(0, NP - 1)], g_recv.at[which])


def per_device(queries, keys, values, teacher, query_map, key_map):
    def flat(a):
        return a.reshape(-1, DH)

    def dma(*shape):
        return pltpu.SemaphoreType.DMA(shape)

    out = pl.pallas_call(
        kernel,
        out_shape=jax.ShapeDtypeStruct((2, NP, 8, DH), F32),
        in_specs=[pl.BlockSpec(memory_space=pl.ANY)] * 6,
        out_specs=pl.BlockSpec(memory_space=pl.ANY),
        scratch_shapes=[
            pltpu.VMEM((4, 4 * TOK, DH), BF16),
            pltpu.VMEM((2, DH, DH), BF16),
            pltpu.VMEM((4, 4 * TOK, DH), F32),
            pltpu.VMEM((3, 4, TOK, DH), F32),
            pltpu.VMEM((3, NX, TOK, DH), F32),
            pltpu.VMEM((2, 4, HALF, TOK), F32),
            pltpu.VMEM((2, NX, HALF, TOK), F32),
            pltpu.VMEM((NZ, FC + 2, DH), F32),
            pltpu.VMEM((NZ, FC + 2, DH), F32),
            pltpu.VMEM((NZ, FC, DH), F32),
            pltpu.VMEM((NZ, FC, DH), F32),
            pltpu.VMEM((2, NZ, FC + 1, DH), F32),
            pltpu.VMEM((2, NZ, FC + 1, DH), F32),
            pltpu.VMEM((2, 2, NZ, FC, DH), F32),
            pltpu.VMEM((2, 2, NZ, FC, DH), F32),
            pltpu.VMEM((2, NP, 8, DH), F32),
            pltpu.VMEM((2, NP * NC, 8, DH), F32),
            pltpu.VMEM((2, 2, 8, DH), F32),
            pltpu.VMEM((2, NZ, 8, DH), F32),
            dma(6),
            dma(5),
            dma(5),
            dma(8),
            dma(8),
            dma(2),
            dma(2),
            dma(2),
            dma(2),
            dma(2),
            dma(2),
            dma(2),
            pltpu.SemaphoreType.REGULAR,
            pltpu.SemaphoreType.REGULAR,
            pltpu.SemaphoreType.REGULAR,
            pltpu.SemaphoreType.REGULAR,
        ],
        compiler_params=pltpu.CompilerParams(
            collective_id=0, has_side_effects=True, vmem_limit_bytes=56 * 1024 * 1024
        ),
        name="hedgehog",
    )(flat(keys), flat(values), flat(queries), flat(teacher), query_map, key_map)
    return out[0].reshape(DH, DH), out[1].reshape(DH, DH)


def solution(mesh):
    split_spec = P(None, "seq", "head", None)
    return jax.shard_map(
        per_device,
        mesh=mesh,
        in_specs=(split_spec,) * 4 + (P(), P()),
        out_specs=(P(), P()),
        check_vma=False,
    )
```

```python
import jax
import jax.numpy as jnp
from jax import lax
from jax.experimental import pallas as pl
from jax.experimental.pallas import tpu as pltpu
from jax.sharding import PartitionSpec as P

MESH = pl.DeviceIdType.MESH
F32 = jnp.float32
BF16 = jnp.bfloat16

NZ, NX, NY, NC = 16, 4, 4, 2
TOK = 128
DH = 128
F2 = 256
LOC = NX * TOK
FC = DH // NZ
Z_FAR = (8, 7, 9, 6, 10, 5, 11)
Z_NEAR = (4, 12, 3, 13, 2, 14, 1, 15)
Z_FAR_FIRST = Z_FAR + Z_NEAR
X_FAR_FIRST = (2, 1, 3)
PLANE_FAR_FIRST = tuple(
    sorted(
        ((dx, dy, dc) for dx in range(NX) for dy in range(NY) for dc in range(NC) if dx or dy or dc),
        key=lambda d: -(min(d[0], NX - d[0]) + min(d[1], NY - d[1])),
    )
)
NP = NX * NY
HALF = DH // 2

NN = (((1,), (0,)), ((), ()))
NT = (((1,), (1,)), ((), ()))
TN = (((0,), (0,)), ((), ()))


def split(a):
    high = a.astype(BF16)
    return high, (a - high.astype(F32)).astype(BF16)


def mm(a, b, dims):
    return lax.dot_general(a, b, dims, preferred_element_type=F32)


def mm3(a, b, dims):
    return mm(a[0], b[0], dims) + (mm(a[0], b[1], dims) + mm(a[1], b[0], dims))


def mm2(a, b, dims):
    return mm(a[0], b, dims) + mm(a[1], b, dims)


def mm_wide(a, b):
    both = mm(a, b, NN)
    return both[:, :DH] + both[:, DH:]


def side(pair):
    return jnp.concatenate(pair, 1)


def feature(inputs, matrix):
    logits = mm(inputs, matrix, NN)
    rising = jnp.exp(logits)
    falling = jnp.exp(-logits)
    return jnp.concatenate(
        [
            rising / jnp.sum(rising, -1, keepdims=True),
            falling / jnp.sum(falling, -1, keepdims=True),
        ],
        -1,
    )


def feature_back(phi, dphi):
    return phi * (dphi - jnp.sum(phi * dphi, -1, keepdims=True))


def kernel(
    k_hbm,
    v_hbm,
    q_hbm,
    t_hbm,
    qmap_hbm,
    kmap_hbm,
    out_ref,
    raw,
    maps,
    wide,
    stage,
    held,
    stage_v,
    held_v,
    state_a,
    got_state_a,
    state_b,
    got_state_b,
    state_c,
    got_state_c,
    totals,
    entering,
    part,
    got_part,
    sums,
    got_sum,
    load_sem,
    x_send,
    x_recv,
    z_send,
    z_recv,
    r_send,
    r_recv,
    s_send,
    s_recv,
    g_send,
    g_recv,
    own_sem,
    near_sem,
    far_sem,
    row_sem,
    plane_sem,
):
    seq, head = lax.axis_index("seq"), lax.axis_index("head")
    z, x = seq // NX, seq % NX
    y, core = head // NC, head % NC

    def at_z(d):
        other = (z + d) % NZ
        return other, (other * NX + x, head)

    def at_x(d):
        other = (x + d) % NX
        return other, (z * NX + other, head)

    def at_plane(d):
        ox, oy, oc = (x + d[0]) % NX, (y + d[1]) % NY, (core + d[2]) % NC
        return ox * NY + oy, (z * NX + ox, oy * NC + oc)

    def signal(sem, device):
        pl.semaphore_signal(sem, inc=1, device_id=device, device_id_type=MESH)

    def send(src, dst, send_sem, recv_sem, device):
        pltpu.make_async_remote_copy(
            src_ref=src,
            dst_ref=dst,
            send_sem=send_sem,
            recv_sem=recv_sem,
            device_id=device,
            device_id_type=MESH,
        ).start()

    def wait(ref, sem):
        pltpu.make_async_copy(ref, ref, sem).wait()

    barrier = pltpu.get_barrier_semaphore()
    near = [at_x(d)[1] for d in X_FAR_FIRST]
    near += [at_z(d)[1] for d in (2, NZ - 2, 1, NZ - 1)]
    near += [at_plane((0, d, 0))[1] for d in (2, 1, 3)]
    near += [at_plane((0, 0, 1))[1]]
    for device in near:
        signal(barrier, device)

    loads = []
    for i, (src, dst) in enumerate(
        (
            (k_hbm, raw.at[0]),
            (v_hbm, raw.at[1]),
            (q_hbm, raw.at[2]),
            (t_hbm, raw.at[3]),
            (kmap_hbm, maps.at[0]),
            (qmap_hbm, maps.at[1]),
        )
    ):
        load = pltpu.make_async_copy(src, dst, load_sem.at[i])
        load.start()
        loads.append(load)

    def widen(i, source):
        wide[source] = raw[source].astype(F32)
        for b in range(2):
            for h in range(2):
                stage[i, b * 2 + h] = wide[source, pl.ds(b * 2 * TOK + h, TOK, stride=2), :]
        held[i, x] = stage[i, x]

    def widen_v():
        wide[1] = raw[1].astype(F32)
        for b in range(2):
            for h in range(2):
                turned = wide[1, pl.ds(b * 2 * TOK + h, TOK, stride=2), :].T
                for half in range(2):
                    stage_v[half, b * 2 + h] = turned[half * HALF : (half + 1) * HALF]
        for half in range(2):
            held_v[half, x] = stage_v[half, x]

    def send_x(i):
        for d in X_FAR_FIRST:
            other, device = at_x(d)
            send(stage.at[i, other], held.at[i, x], x_send.at[i], x_recv.at[i], device)

    def send_v(half):
        for d in X_FAR_FIRST:
            other, device = at_x(d)
            send(stage_v.at[half, other], held_v.at[half, x], x_send.at[3 + half], x_recv.at[3 + half], device)

    loads[0].wait()
    widen(0, 0)
    loads[1].wait()
    widen_v()
    pl.semaphore_wait(barrier, len(near))
    send_x(0)
    send_v(0)
    send_v(1)
    for d in (2, NZ - 2):
        signal(near_sem, at_z(d)[1])
    for d in (2, 1, 3):
        signal(row_sem, at_plane((0, d, 0))[1])
    loads[2].wait()
    widen(1, 2)
    loads[3].wait()
    widen(2, 3)
    loads[4].wait()
    loads[5].wait()
    pl.semaphore_wait(near_sem, 2)
    for d in (4, NZ - 4):
        signal(far_sem, at_z(d)[1])
    pl.semaphore_wait(row_sem, 3)
    signal(plane_sem, at_plane((0, 0, 1))[1])

    def receive_x(i):
        wait(held.at[i, pl.ds(0, NX - 1)], x_recv.at[i])
        return held[i].reshape(LOC, DH)

    def receive_v(half):
        wait(held_v.at[half, pl.ds(0, NX - 1)], x_recv.at[3 + half])
        return jnp.concatenate([held_v[half, i] for i in range(NX)], 1).astype(BF16)

    streams = (
        ((state_a, got_state_a), (state_b, got_state_b)),
        tuple((state_c.at[sign], got_state_c.at[sign]) for sign in range(2)),
    )

    def scatter_z(scan, stream):
        rows, got = streams[scan][stream]
        got[z] = rows[z]
        send_rows(scan, stream, Z_FAR)

    def send_rows(scan, stream, distances):
        rows, got = streams[scan][stream]
        sem = 4 * scan + stream
        for d in distances:
            other, device = at_z(d)
            send(rows.at[other], got.at[z], z_send.at[sem], z_recv.at[sem], device)

    def return_z(scan, stream, reverse):
        got = streams[scan][stream][1]
        sem = 4 * scan + stream
        wait(got.at[pl.ds(0, NZ - 1)], z_recv.at[sem])
        order = range(NZ - 1, -1, -1) if reverse else range(NZ)
        running = jnp.zeros((FC, DH), F32)
        for one in order:
            totals[scan, stream, one] = running
            running = running + got[one, :FC, :]
        entering[scan, stream, z] = totals[scan, stream, z]
        send_totals(scan, stream, Z_FAR)

    def send_totals(scan, stream, distances):
        sem = 4 * scan + stream + 2
        for d in distances:
            other, device = at_z(d)
            send(totals.at[scan, stream, other], entering.at[scan, stream, z], z_send.at[sem], z_recv.at[sem], device)

    def norm_z(got, row, reverse):
        norm = jnp.zeros((1, DH), F32)
        for one in range(NZ):
            before = one > z if reverse else one < z
            norm = norm + jnp.where(before, got[one, row : row + 1, :], 0.0)
        return norm

    def receive_z(scan, stream):
        wait(entering.at[scan, stream, pl.ds(0, NZ - 1)], z_recv.at[4 * scan + stream + 2])
        return entering[scan, stream]

    mine = x * NY + y

    def reduce_plane(which, grad):
        if which == 0:
            pl.semaphore_wait(plane_sem, 1)
        part[which] = grad.reshape(NP, 8, DH)
        for d in sorted(PLANE_FAR_FIRST, key=lambda d: d[2]):
            other, device = at_plane(d)
            send(part.at[which, other], got_part.at[which, mine * NC + core], r_send.at[which], r_recv.at[which], device)
        got_part[which, mine * NC + core] = part[which, mine]

    def reduce_z(which):
        wait(got_part.at[which, pl.ds(0, NP * NC - 1)], r_recv.at[which])
        sums[which, 0] = jnp.sum(got_part[which], 0)
        for d in Z_FAR_FIRST:
            send(sums.at[which, 0], got_sum.at[which, z], s_send.at[which], s_recv.at[which], at_z(d)[1])
        got_sum[which, z] = sums[which, 0]

    def share(which):
        wait(got_sum.at[which, pl.ds(0, NZ - 1)], s_recv.at[which])
        sums[which, 1] = jnp.sum(got_sum[which], 0)
        for d in PLANE_FAR_FIRST:
            if not d[2]:
                send(sums.at[which, 1], out_ref.at[which, mine], g_send.at[which], g_recv.at[which], at_plane(d)[1])
        pltpu.make_async_copy(sums.at[which, 1], out_ref.at[which, mine], own_sem.at[which]).start()

    keys = receive_x(0).astype(BF16)
    key_phi = feature(keys, maps[0])
    kphi = split(key_phi)
    key_sum = jnp.sum(key_phi, 0, keepdims=True)
    for i in range(2):
        state_a[:, FC + i, :] = jnp.broadcast_to(key_sum[:, i * DH : (i + 1) * DH], (NZ, DH))
    values_t = []
    for half in range(2):
        values_t.append(receive_v(half))
        local = mm(values_t[half], kphi[0], NN) + mm(values_t[half], kphi[1], NN)
        rows = streams[0][half][0]
        for owner in range(NZ):
            i, j = owner // 2, owner % 2
            rows[owner, :FC, :] = local[i * FC : (i + 1) * FC, j * DH : (j + 1) * DH]
        if half == 0:
            pl.semaphore_wait(far_sem, 2)
        scatter_z(0, half)
    for half in range(2):
        send_rows(0, half, Z_NEAR)
    send_x(1)
    send_x(2)
    values_t = jnp.concatenate(values_t, 0)
    values = values_t.T

    for half in range(2):
        return_z(0, half, False)
    for half in range(2):
        send_totals(0, half, Z_NEAR)
    prefix_norm = side([norm_z(got_state_a, FC + i, False) for i in range(2)])
    queries = receive_x(1).astype(BF16)
    query_phi = feature(queries, maps[1])
    qphi = split(query_phi)

    causal = lax.broadcasted_iota(jnp.int32, (LOC, LOC), 0) >= lax.broadcasted_iota(
        jnp.int32, (LOC, LOC), 1
    )
    scores = jnp.where(causal, mm3(qphi, kphi, NT), 0.0)
    inner_num = mm2(split(scores), values, NN)
    denominator = jnp.sum(scores, 1, keepdims=True) + jnp.sum(query_phi * prefix_norm, 1, keepdims=True)
    target = receive_x(2)
    qphi_t = tuple(a.T for a in qphi)
    keys_t = keys.T

    prefix = []
    for half in range(2):
        blocks = receive_z(0, half)
        for i in range(NZ // 2):
            prefix.append(side([blocks[2 * i], blocks[2 * i + 1]]))
    prefix = split(jnp.concatenate(prefix, 0))
    both = mm(qphi[0], jnp.concatenate(prefix, 0), NT)
    numerator = inner_num + (both[:, :DH] + (both[:, DH:] + mm(qphi[1], prefix[0], NT)))
    output = numerator / denominator
    misfit = output - target
    grad_num = misfit / denominator
    grad_den = -jnp.sum(misfit * output, 1, keepdims=True) / denominator
    gnum = split(grad_num)
    gnum_side = side(gnum)
    query_sum = jnp.sum(query_phi * grad_den, 0, keepdims=True)
    for sign in range(2):
        lanes = slice(sign * DH, (sign + 1) * DH)
        back = mm_wide(qphi_t[0][lanes], gnum_side) + mm(qphi_t[1][lanes], gnum[0], NN)
        state_c[sign, :, :FC, :] = back.reshape(NZ, FC, DH)
        state_c[sign, :, FC, :] = jnp.broadcast_to(query_sum[:, lanes], (NZ, DH))
        scatter_z(1, sign)
    for sign in range(2):
        send_rows(1, sign, Z_NEAR)

    mixed = split(jnp.where(causal, mm2(gnum, values, NT) + grad_den, 0.0))
    query_dphi = mm3(mixed, kphi, NN) + mm3(gnum, prefix, NN) + grad_den * prefix_norm
    grad_aq = split(
        feature_back(query_phi[:, :DH], query_dphi[:, :DH]) - feature_back(query_phi[:, DH:], query_dphi[:, DH:])
    )
    reduce_plane(0, mm_wide(queries.T, side(grad_aq)))
    key_inner = mm3(mixed, qphi, TN)

    for sign in range(2):
        return_z(1, sign, True)
    for sign in range(2):
        send_totals(1, sign, Z_NEAR)
    suffix_norm = side([norm_z(got_state_c.at[sign], FC, True) for sign in range(2)])
    key_inner = key_inner + suffix_norm
    reduce_z(0)
    grad_ak = []
    for sign in range(2):
        suffix = split(receive_z(1, sign).reshape(DH, DH))
        lanes = slice(sign * DH, (sign + 1) * DH)
        both = mm(values, jnp.concatenate(suffix, 0), NT)
        grad_ak.append(feature_back(key_phi[:, lanes], key_inner[:, lanes] + (both[:, :DH] + both[:, DH:])))
    reduce_plane(1, mm_wide(keys_t, side(split(grad_ak[0] - grad_ak[1]))))
    reduce_z(1)
    share(0)
    share(1)

    for i in range(3):
        wait(held.at[i, pl.ds(0, NX - 1)], x_send.at[i])
    for half in range(2):
        wait(held_v.at[half, pl.ds(0, NX - 1)], x_send.at[3 + half])
    for scan in range(2):
        for stream in range(2):
            rows = streams[scan][stream][0]
            wait(rows.at[pl.ds(0, NZ - 1)], z_send.at[4 * scan + stream])
            wait(totals.at[scan, stream, pl.ds(0, NZ - 1)], z_send.at[4 * scan + stream + 2])
    for which in range(2):
        wait(got_part.at[which, pl.ds(0, NP * NC - 1)], r_send.at[which])
        wait(got_sum.at[which, pl.ds(0, NZ - 1)], s_send.at[which])
        wait(got_part.at[which, pl.ds(0, NP - 1)], g_send.at[which])
        wait(sums.at[which, 1], own_sem.at[which])
        wait(out_ref.at[which, pl.ds(0, NP - 1)], g_recv.at[which])


def per_device(queries, keys, values, teacher, query_map, key_map):
    def flat(a):
        return a.reshape(-1, DH)

    def dma(*shape):
        return pltpu.SemaphoreType.DMA(shape)

    out = pl.pallas_call(
        kernel,
        out_shape=jax.ShapeDtypeStruct((2, NP, 8, DH), F32),
        in_specs=[pl.BlockSpec(memory_space=pl.ANY)] * 6,
        out_specs=pl.BlockSpec(memory_space=pl.ANY),
        scratch_shapes=[
            pltpu.VMEM((4, 4 * TOK, DH), BF16),
            pltpu.VMEM((2, DH, DH), BF16),
            pltpu.VMEM((4, 4 * TOK, DH), F32),
            pltpu.VMEM((3, 4, TOK, DH), F32),
            pltpu.VMEM((3, NX, TOK, DH), F32),
            pltpu.VMEM((2, 4, HALF, TOK), F32),
            pltpu.VMEM((2, NX, HALF, TOK), F32),
            pltpu.VMEM((NZ, FC + 2, DH), F32),
            pltpu.VMEM((NZ, FC + 2, DH), F32),
            pltpu.VMEM((NZ, FC, DH), F32),
            pltpu.VMEM((NZ, FC, DH), F32),
            pltpu.VMEM((2, NZ, FC + 1, DH), F32),
            pltpu.VMEM((2, NZ, FC + 1, DH), F32),
            pltpu.VMEM((2, 2, NZ, FC, DH), F32),
            pltpu.VMEM((2, 2, NZ, FC, DH), F32),
            pltpu.VMEM((2, NP, 8, DH), F32),
            pltpu.VMEM((2, NP * NC, 8, DH), F32),
            pltpu.VMEM((2, 2, 8, DH), F32),
            pltpu.VMEM((2, NZ, 8, DH), F32),
            dma(6),
            dma(5),
            dma(5),
            dma(8),
            dma(8),
            dma(2),
            dma(2),
            dma(2),
            dma(2),
            dma(2),
            dma(2),
            dma(2),
            pltpu.SemaphoreType.REGULAR,
            pltpu.SemaphoreType.REGULAR,
            pltpu.SemaphoreType.REGULAR,
            pltpu.SemaphoreType.REGULAR,
        ],
        compiler_params=pltpu.CompilerParams(
            collective_id=0, has_side_effects=True, vmem_limit_bytes=56 * 1024 * 1024
        ),
        name="hedgehog",
    )(flat(keys), flat(values), flat(queries), flat(teacher), query_map, key_map)
    return out[0].reshape(DH, DH), out[1].reshape(DH, DH)


def solution(mesh):
    split_spec = P(None, "seq", "head", None)
    return jax.shard_map(
        per_device,
        mesh=mesh,
        in_specs=(split_spec,) * 4 + (P(), P()),
        out_specs=(P(), P()),
        check_vma=False,
    )
```

```python
import jax
import jax.numpy as jnp
from jax import lax
from jax.experimental import pallas as pl
from jax.experimental.pallas import tpu as pltpu
from jax.sharding import PartitionSpec as P

MESH = pl.DeviceIdType.MESH
F32 = jnp.float32
BF16 = jnp.bfloat16

NZ, NX, NY, NC = 16, 4, 4, 2
TOK = 128
DH = 128
F2 = 256
LOC = NX * TOK
FC = DH // NZ
Z_FAR = (8, 7, 9, 6, 10, 5, 11)
Z_NEAR = (4, 12, 3, 13, 2, 14, 1, 15)
Z_FAR_FIRST = Z_FAR + Z_NEAR
X_FAR_FIRST = (2, 1, 3)
PLANE_FAR_FIRST = tuple(
    sorted(
        ((dx, dy, dc) for dx in range(NX) for dy in range(NY) for dc in range(NC) if dx or dy or dc),
        key=lambda d: -(min(d[0], NX - d[0]) + min(d[1], NY - d[1])),
    )
)
NP = NX * NY
HALF = DH // 2

NN = (((1,), (0,)), ((), ()))
NT = (((1,), (1,)), ((), ()))
TN = (((0,), (0,)), ((), ()))


def split(a):
    high = a.astype(BF16)
    return high, (a - high.astype(F32)).astype(BF16)


def mm(a, b, dims):
    return lax.dot_general(a, b, dims, preferred_element_type=F32)


def mm3(a, b, dims):
    return mm(a[0], b[0], dims) + (mm(a[0], b[1], dims) + mm(a[1], b[0], dims))


def mm2(a, b, dims):
    return mm(a[0], b, dims) + mm(a[1], b, dims)


def mm_wide(a, b):
    both = mm(a, b, NN)
    return both[:, :DH] + both[:, DH:]


def side(pair):
    return jnp.concatenate(pair, 1)


def feature(inputs, matrix):
    logits = mm(inputs, matrix, NN)
    rising = jnp.exp(logits)
    falling = jnp.exp(-logits)
    return jnp.concatenate(
        [
            rising / jnp.sum(rising, -1, keepdims=True),
            falling / jnp.sum(falling, -1, keepdims=True),
        ],
        -1,
    )


def feature_back(phi, dphi):
    return phi * (dphi - jnp.sum(phi * dphi, -1, keepdims=True))


def kernel(
    k_hbm,
    v_hbm,
    q_hbm,
    t_hbm,
    qmap_hbm,
    kmap_hbm,
    out_ref,
    raw,
    maps,
    wide,
    stage,
    held,
    stage_v,
    held_v,
    state_a,
    got_state_a,
    state_b,
    got_state_b,
    state_c,
    got_state_c,
    totals,
    entering,
    part,
    got_part,
    sums,
    got_sum,
    load_sem,
    x_send,
    x_recv,
    z_send,
    z_recv,
    r_send,
    r_recv,
    s_send,
    s_recv,
    g_send,
    g_recv,
    own_sem,
    near_sem,
    far_sem,
    row_sem,
    plane_sem,
):
    seq, head = lax.axis_index("seq"), lax.axis_index("head")
    z, x = seq // NX, seq % NX
    y, core = head // NC, head % NC

    def at_z(d):
        other = (z + d) % NZ
        return other, (other * NX + x, head)

    def at_x(d):
        other = (x + d) % NX
        return other, (z * NX + other, head)

    def at_plane(d):
        ox, oy, oc = (x + d[0]) % NX, (y + d[1]) % NY, (core + d[2]) % NC
        return ox * NY + oy, (z * NX + ox, oy * NC + oc)

    def signal(sem, device):
        pl.semaphore_signal(sem, inc=1, device_id=device, device_id_type=MESH)

    def send(src, dst, send_sem, recv_sem, device):
        pltpu.make_async_remote_copy(
            src_ref=src,
            dst_ref=dst,
            send_sem=send_sem,
            recv_sem=recv_sem,
            device_id=device,
            device_id_type=MESH,
        ).start()

    def wait(ref, sem):
        pltpu.make_async_copy(ref, ref, sem).wait()

    barrier = pltpu.get_barrier_semaphore()
    near = [at_x(d)[1] for d in X_FAR_FIRST]
    near += [at_z(d)[1] for d in (2, NZ - 2, 1, NZ - 1)]
    near += [at_plane((0, d, 0))[1] for d in (2, 1, 3)]
    near += [at_plane((0, 0, 1))[1]]
    for device in near:
        signal(barrier, device)

    loads = []
    for i, (src, dst) in enumerate(
        (
            (k_hbm, raw.at[0]),
            (v_hbm, raw.at[1]),
            (q_hbm, raw.at[2]),
            (t_hbm, raw.at[3]),
            (kmap_hbm, maps.at[0]),
            (qmap_hbm, maps.at[1]),
        )
    ):
        load = pltpu.make_async_copy(src, dst, load_sem.at[i])
        load.start()
        loads.append(load)

    def widen(i, source):
        wide[source] = raw[source].astype(F32)
        for b in range(2):
            for h in range(2):
                stage[i, b * 2 + h] = wide[source, pl.ds(b * 2 * TOK + h, TOK, stride=2), :]
        held[i, x] = stage[i, x]

    def widen_v():
        wide[1] = raw[1].astype(F32)
        for b in range(2):
            for h in range(2):
                turned = wide[1, pl.ds(b * 2 * TOK + h, TOK, stride=2), :].T
                for half in range(2):
                    stage_v[half, b * 2 + h] = turned[half * HALF : (half + 1) * HALF]
        for half in range(2):
            held_v[half, x] = stage_v[half, x]

    def send_x(i):
        for d in X_FAR_FIRST:
            other, device = at_x(d)
            send(stage.at[i, other], held.at[i, x], x_send.at[i], x_recv.at[i], device)

    def send_v(half):
        for d in X_FAR_FIRST:
            other, device = at_x(d)
            send(stage_v.at[half, other], held_v.at[half, x], x_send.at[3 + half], x_recv.at[3 + half], device)

    loads[0].wait()
    widen(0, 0)
    loads[1].wait()
    widen_v()
    pl.semaphore_wait(barrier, len(near))
    send_x(0)
    send_v(0)
    send_v(1)
    for d in (2, NZ - 2):
        signal(near_sem, at_z(d)[1])
    for d in (2, 1, 3):
        signal(row_sem, at_plane((0, d, 0))[1])
    loads[2].wait()
    widen(1, 2)
    loads[3].wait()
    widen(2, 3)
    loads[4].wait()
    loads[5].wait()
    pl.semaphore_wait(near_sem, 2)
    for d in (4, NZ - 4):
        signal(far_sem, at_z(d)[1])
    pl.semaphore_wait(row_sem, 3)
    signal(plane_sem, at_plane((0, 0, 1))[1])

    def receive_x(i):
        wait(held.at[i, pl.ds(0, NX - 1)], x_recv.at[i])
        return held[i].reshape(LOC, DH)

    def receive_v(half):
        wait(held_v.at[half, pl.ds(0, NX - 1)], x_recv.at[3 + half])
        return jnp.concatenate([held_v[half, i] for i in range(NX)], 1).astype(BF16)

    streams = (
        ((state_a, got_state_a), (state_b, got_state_b)),
        tuple((state_c.at[sign], got_state_c.at[sign]) for sign in range(2)),
    )

    def scatter_z(scan, stream):
        rows, got = streams[scan][stream]
        got[z] = rows[z]
        send_rows(scan, stream, Z_FAR)

    def send_rows(scan, stream, distances):
        rows, got = streams[scan][stream]
        sem = 4 * scan + stream
        for d in distances:
            other, device = at_z(d)
            send(rows.at[other], got.at[z], z_send.at[sem], z_recv.at[sem], device)

    def return_z(scan, stream, reverse):
        got = streams[scan][stream][1]
        sem = 4 * scan + stream
        wait(got.at[pl.ds(0, NZ - 1)], z_recv.at[sem])
        order = range(NZ - 1, -1, -1) if reverse else range(NZ)
        running = jnp.zeros((FC, DH), F32)
        for one in order:
            totals[scan, stream, one] = running
            running = running + got[one, :FC, :]
        entering[scan, stream, z] = totals[scan, stream, z]
        send_totals(scan, stream, Z_FAR)

    def send_totals(scan, stream, distances):
        sem = 4 * scan + stream + 2
        for d in distances:
            other, device = at_z(d)
            send(totals.at[scan, stream, other], entering.at[scan, stream, z], z_send.at[sem], z_recv.at[sem], device)

    def norm_z(got, row, reverse):
        norm = jnp.zeros((1, DH), F32)
        for one in range(NZ):
            before = one > z if reverse else one < z
            norm = norm + jnp.where(before, got[one, row : row + 1, :], 0.0)
        return norm

    def receive_z(scan, stream):
        wait(entering.at[scan, stream, pl.ds(0, NZ - 1)], z_recv.at[4 * scan + stream + 2])
        return entering[scan, stream]

    mine = x * NY + y

    def reduce_plane(which, grad):
        if which == 0:
            pl.semaphore_wait(plane_sem, 1)
        part[which] = grad.reshape(NP, 8, DH)
        for d in sorted(PLANE_FAR_FIRST, key=lambda d: d[2]):
            other, device = at_plane(d)
            send(part.at[which, other], got_part.at[which, mine * NC + core], r_send.at[which], r_recv.at[which], device)
        got_part[which, mine * NC + core] = part[which, mine]

    def reduce_z(which):
        wait(got_part.at[which, pl.ds(0, NP * NC - 1)], r_recv.at[which])
        sums[which, 0] = jnp.sum(got_part[which], 0)
        for d in Z_FAR_FIRST:
            send(sums.at[which, 0], got_sum.at[which, z], s_send.at[which], s_recv.at[which], at_z(d)[1])
        got_sum[which, z] = sums[which, 0]

    def share(which):
        wait(got_sum.at[which, pl.ds(0, NZ - 1)], s_recv.at[which])
        sums[which, 1] = jnp.sum(got_sum[which], 0)
        for d in PLANE_FAR_FIRST:
            if not d[2]:
                send(sums.at[which, 1], out_ref.at[which, mine], g_send.at[which], g_recv.at[which], at_plane(d)[1])
        pltpu.make_async_copy(sums.at[which, 1], out_ref.at[which, mine], own_sem.at[which]).start()

    keys = receive_x(0).astype(BF16)
    key_phi = feature(keys, maps[0])
    kphi = split(key_phi)
    key_sum = jnp.sum(key_phi, 0, keepdims=True)
    for i in range(2):
        state_a[:, FC + i, :] = jnp.broadcast_to(key_sum[:, i * DH : (i + 1) * DH], (NZ, DH))
    values_t = []
    for half in range(2):
        values_t.append(receive_v(half))
        local = mm(values_t[half], kphi[0], NN) + mm(values_t[half], kphi[1], NN)
        rows = streams[0][half][0]
        for owner in range(NZ):
            i, j = owner // 2, owner % 2
            rows[owner, :FC, :] = local[i * FC : (i + 1) * FC, j * DH : (j + 1) * DH]
        if half == 0:
            pl.semaphore_wait(far_sem, 2)
        scatter_z(0, half)
    for half in range(2):
        send_rows(0, half, Z_NEAR)
    send_x(1)
    send_x(2)
    values_t = jnp.concatenate(values_t, 0)
    values = values_t.T

    for half in range(2):
        return_z(0, half, False)
    for half in range(2):
        send_totals(0, half, Z_NEAR)
    prefix_norm = side([norm_z(got_state_a, FC + i, False) for i in range(2)])
    queries = receive_x(1).astype(BF16)
    query_phi = feature(queries, maps[1])
    qphi = split(query_phi)

    causal = lax.broadcasted_iota(jnp.int32, (LOC, LOC), 0) >= lax.broadcasted_iota(
        jnp.int32, (LOC, LOC), 1
    )
    scores = jnp.where(causal, mm3(qphi, kphi, NT), 0.0)
    inner_num = mm2(split(scores), values, NN)
    denominator = jnp.sum(scores, 1, keepdims=True) + jnp.sum(query_phi * prefix_norm, 1, keepdims=True)
    target = receive_x(2)
    qphi_t = tuple(a.T for a in qphi)
    keys_t = keys.T

    prefix = []
    for half in range(2):
        blocks = receive_z(0, half)
        for i in range(NZ // 2):
            prefix.append(side([blocks[2 * i], blocks[2 * i + 1]]))
    prefix = split(jnp.concatenate(prefix, 0))
    both = mm(qphi[0], jnp.concatenate(prefix, 0), NT)
    numerator = inner_num + (both[:, :DH] + (both[:, DH:] + mm(qphi[1], prefix[0], NT)))
    output = numerator / denominator
    misfit = output - target
    grad_num = misfit / denominator
    grad_den = -jnp.sum(misfit * output, 1, keepdims=True) / denominator
    gnum = split(grad_num)
    gnum_side = side(gnum)
    for sign in range(2):
        lanes = slice(sign * DH, (sign + 1) * DH)
        back = mm_wide(qphi_t[0][lanes], gnum_side) + mm(qphi_t[1][lanes], gnum[0], NN)
        state_c[sign, :, :FC, :] = back.reshape(NZ, FC, DH)
        query_sum = jnp.sum(query_phi[:, lanes] * grad_den, 0, keepdims=True)
        state_c[sign, :, FC, :] = jnp.broadcast_to(query_sum, (NZ, DH))
        scatter_z(1, sign)
    for sign in range(2):
        send_rows(1, sign, Z_NEAR)

    mixed = split(jnp.where(causal, mm2(gnum, values, NT) + grad_den, 0.0))
    query_dphi = mm3(mixed, kphi, NN) + mm3(gnum, prefix, NN) + grad_den * prefix_norm
    grad_aq = split(
        feature_back(query_phi[:, :DH], query_dphi[:, :DH]) - feature_back(query_phi[:, DH:], query_dphi[:, DH:])
    )
    reduce_plane(0, mm_wide(queries.T, side(grad_aq)))
    key_inner = mm3(mixed, qphi, TN)

    for sign in range(2):
        return_z(1, sign, True)
    for sign in range(2):
        send_totals(1, sign, Z_NEAR)
    suffix_norm = side([norm_z(got_state_c.at[sign], FC, True) for sign in range(2)])
    key_inner = key_inner + suffix_norm
    reduce_z(0)
    grad_ak = []
    for sign in range(2):
        suffix = split(receive_z(1, sign).reshape(DH, DH))
        lanes = slice(sign * DH, (sign + 1) * DH)
        both = mm(values, jnp.concatenate(suffix, 0), NT)
        grad_ak.append(feature_back(key_phi[:, lanes], key_inner[:, lanes] + (both[:, :DH] + both[:, DH:])))
    reduce_plane(1, mm_wide(keys_t, side(split(grad_ak[0] - grad_ak[1]))))
    reduce_z(1)
    share(0)
    share(1)

    for i in range(3):
        wait(held.at[i, pl.ds(0, NX - 1)], x_send.at[i])
    for half in range(2):
        wait(held_v.at[half, pl.ds(0, NX - 1)], x_send.at[3 + half])
    for scan in range(2):
        for stream in range(2):
            rows = streams[scan][stream][0]
            wait(rows.at[pl.ds(0, NZ - 1)], z_send.at[4 * scan + stream])
            wait(totals.at[scan, stream, pl.ds(0, NZ - 1)], z_send.at[4 * scan + stream + 2])
    for which in range(2):
        wait(got_part.at[which, pl.ds(0, NP * NC - 1)], r_send.at[which])
        wait(got_sum.at[which, pl.ds(0, NZ - 1)], s_send.at[which])
        wait(got_part.at[which, pl.ds(0, NP - 1)], g_send.at[which])
        wait(sums.at[which, 1], own_sem.at[which])
        wait(out_ref.at[which, pl.ds(0, NP - 1)], g_recv.at[which])


def per_device(queries, keys, values, teacher, query_map, key_map):
    def flat(a):
        return a.reshape(-1, DH)

    def dma(*shape):
        return pltpu.SemaphoreType.DMA(shape)

    out = pl.pallas_call(
        kernel,
        out_shape=jax.ShapeDtypeStruct((2, NP, 8, DH), F32),
        in_specs=[pl.BlockSpec(memory_space=pl.ANY)] * 6,
        out_specs=pl.BlockSpec(memory_space=pl.ANY),
        scratch_shapes=[
            pltpu.VMEM((4, 4 * TOK, DH), BF16),
            pltpu.VMEM((2, DH, DH), BF16),
            pltpu.VMEM((4, 4 * TOK, DH), F32),
            pltpu.VMEM((3, 4, TOK, DH), F32),
            pltpu.VMEM((3, NX, TOK, DH), F32),
            pltpu.VMEM((2, 4, HALF, TOK), F32),
            pltpu.VMEM((2, NX, HALF, TOK), F32),
            pltpu.VMEM((NZ, FC + 2, DH), F32),
            pltpu.VMEM((NZ, FC + 2, DH), F32),
            pltpu.VMEM((NZ, FC, DH), F32),
            pltpu.VMEM((NZ, FC, DH), F32),
            pltpu.VMEM((2, NZ, FC + 1, DH), F32),
            pltpu.VMEM((2, NZ, FC + 1, DH), F32),
            pltpu.VMEM((2, 2, NZ, FC, DH), F32),
            pltpu.VMEM((2, 2, NZ, FC, DH), F32),
            pltpu.VMEM((2, NP, 8, DH), F32),
            pltpu.VMEM((2, NP * NC, 8, DH), F32),
            pltpu.VMEM((2, 2, 8, DH), F32),
            pltpu.VMEM((2, NZ, 8, DH), F32),
            dma(6),
            dma(5),
            dma(5),
            dma(8),
            dma(8),
            dma(2),
            dma(2),
            dma(2),
            dma(2),
            dma(2),
            dma(2),
            dma(2),
            pltpu.SemaphoreType.REGULAR,
            pltpu.SemaphoreType.REGULAR,
            pltpu.SemaphoreType.REGULAR,
            pltpu.SemaphoreType.REGULAR,
        ],
        compiler_params=pltpu.CompilerParams(
            collective_id=0, has_side_effects=True, vmem_limit_bytes=56 * 1024 * 1024
        ),
        name="hedgehog",
    )(flat(keys), flat(values), flat(queries), flat(teacher), query_map, key_map)
    return out[0].reshape(DH, DH), out[1].reshape(DH, DH)


def solution(mesh):
    split_spec = P(None, "seq", "head", None)
    return jax.shard_map(
        per_device,
        mesh=mesh,
        in_specs=(split_spec,) * 4 + (P(), P()),
        out_specs=(P(), P()),
        check_vma=False,
    )
```
